1024 devices in a mesh: group: 4 (over x), ingroup: 8 (over y, core), hid: 32 (over z).
Axes of the slice: x: 4, y: 4, z: 32, core: 2. Of those that a mesh axis runs over, the one named last changes fastest.
Arguments:
- tokens: bfloat16 [2048, 2048], P(('group', 'hid')), may hold values from -6 to 6
- grad_mixed: bfloat16 [2048, 2048], P(('group', 'hid')), may hold values from -6 to 6
- expert_ids: int32 [2048, 6], P(('group', 'hid')), may hold values from 0 to 63, all different within a row; in each aligned block of 16 rows (0 to 15, 16 to 31, ...) at most 2 rows name the same one
- gate_weight: float32 [2048, 6], P(('group', 'hid')), may hold values from 0.05 to 1
- w_gate: bfloat16 [64, 2048, 1408], P('hid', None, 'ingroup'), may hold values from -0.125 to 0.125
- w_up: bfloat16 [64, 2048, 1408], P('hid', None, 'ingroup'), may hold values from -0.125 to 0.125
- w_down: bfloat16 [64, 1408, 2048], P('hid', 'ingroup'), may hold values from -0.15625 to 0.15625
Outputs:
- mixed: bfloat16 [2048, 2048], P(('group', 'hid'), 'ingroup')
- grad_tokens: bfloat16 [2048, 2048], P(('group', 'hid'), 'ingroup')
- grad_gate: float32 [64, 2048, 1408], P('hid', 'group', 'ingroup')
- grad_up: float32 [64, 2048, 1408], P('hid', 'group', 'ingroup')
- grad_down: float32 [64, 1408, 2048], P('hid', 'ingroup', 'group')
The draws below stay inside these ranges and needn't reach their ends.
Inputs may be any that keep to these rules, and one draw needn't show every extreme that they name: `expert_ids`: each row names 6 different experts. Among the 16 tokens of one index of group and hid (aligned blocks of rows), no expert is named more than 2 times, and that bound is reached.
All inputs are finite; a program needn't handle non-finite values.
Results may differ from the reference program's by a relative error of at most 0.015.
Values may be sent and summed in bfloat16 or wider, within the bound.
A program may use at most 32 MiB of HBM per device.

```python
import math
import jax
import jax.numpy as jnp
import numpy as np
from jax import lax

D = 2048
FF = 1408
EXPERTS = 64
TOP = 6
TOK_DEV = 16
CAP = 2
TOKENS = 2048
N_GROUP = 4
N_INGROUP = 8
N_HID = 32


def levels(stream_key, extent, pieces, low, top_value):
    def one(position, shards_of):
        steps = jax.random.uniform(jax.random.fold_in(jax.random.fold_in(stream_key, 6), position), (shards_of,), jnp.float32, low / len(pieces), top_value / len(pieces))
        return jnp.repeat(jnp.exp(steps), extent[position] // shards_of).reshape((-1,) + (1,) * (len(extent) - position - 1))

    level = one(*pieces[0])
    for cut in pieces[1:]:
        level = level * one(*cut)
    return level


def deal_out(stream_key, own, number, rows, amount, top, bound, slope):
    sequence = jax.random.permutation(stream_key, amount)
    packed, ordinary = load_shares(amount, rows * top, bound, slope, True), load_shares(amount, rows * top, bound, slope, False)
    places = jnp.arange(amount)

    def named(lengths, rotation):
        used = int((lengths > 0).sum())
        fixed = max(1, used // 4)
        moved = fixed + (places - fixed + rotation * (used - fixed)) % max(1, amount - fixed)
        return jnp.zeros((amount,), jnp.int32).at[sequence[jnp.where(places < fixed, places, moved)]].set(jnp.asarray(lengths, jnp.int32))

    lengths = jnp.where(number % 4 == 0, named(packed, number // 4), named(ordinary, number - number // 4 - 1))
    mixed = jax.random.permutation(jax.random.fold_in(own, 3), amount)
    source_of, taker = mixed[0:amount // 2 * 2:2], mixed[1:amount // 2 * 2:2]
    slack = jnp.minimum(lengths[source_of] - 1, bound - lengths[taker]) // 2
    slack = jnp.where((source_of == sequence[0]) | (taker == sequence[0]) | (lengths[taker] == 0), 0, jnp.maximum(slack, 0))
    moved = jax.random.randint(jax.random.fold_in(own, 4), (amount // 2,), 0, 1 << 20) % (slack + 1)
    lengths = lengths.at[source_of].add(-moved).at[taker].add(moved)
    items = jnp.searchsorted(jnp.cumsum(lengths), jnp.arange(rows * top), side="right").astype(jnp.int32)
    table = items.reshape(top, rows).T
    table = table[jax.random.permutation(jax.random.fold_in(own, 1), rows)]
    rotation = jax.random.randint(jax.random.fold_in(own, 2), (rows, 1), 0, top)
    return jnp.take_along_axis(table, (jnp.arange(top)[None, :] + rotation) % top, axis=1)


def load_shares(amount, total, bound, lean, full):
    portions = [(1 << 20) // math.isqrt(grade ** lean) + 1 for grade in range(1, amount + 1)]
    largest = bound if full else min(bound, max(-(-total // amount), total * portions[0] // sum(portions)))
    least = 1 if total - largest >= amount - 1 else 0
    counts, surplus = [largest] + [least] * (amount - 1), total - largest - least * (amount - 1)
    while surplus > 0:
        candidates = [i for i in range(1, amount) if counts[i] < largest] or [i for i in range(1, amount) if counts[i] < bound]
        mass, remaining = sum([portions[i] for i in candidates]), surplus
        for i in candidates:
            addition = min(bound - counts[i], max(1, remaining * portions[i] // mass), surplus)
            counts[i] = counts[i] + addition
            surplus = surplus - addition
    return np.array(counts)


def gaussian(own_key, dims, deviation, most, pieces=(), held_as=jnp.bfloat16):
    array = jax.random.normal(own_key, dims, jnp.float32) * deviation
    if len(pieces) > 0:
        array = levels(own_key, dims, pieces, -0.22, 0.18) * array
    return jnp.clip(array, min=-most, max=most).astype(held_as)


def setup_inputs(seed: int = 0) -> dict:
    key_of = jax.random.split(jax.random.key(seed), 8)
    tokens = gaussian(key_of[0], (TOKENS, D), 1.0, 6.0, ((0, 128),))
    grad_mixed = gaussian(key_of[1], (TOKENS, D), 1.0, 6.0, ((0, 128),))
    expert_ids_keys = jax.random.split(jax.random.fold_in(key_of[2], 1), TOKENS // TOK_DEV)
    expert_ids_turns = jax.random.permutation(jax.random.fold_in(key_of[2], 3), TOKENS // TOK_DEV)
    expert_ids = jax.vmap(lambda own, number: deal_out(jax.random.fold_in(key_of[2], 2), own, number, TOK_DEV, EXPERTS, TOP, CAP, 2))(expert_ids_keys, expert_ids_turns).reshape((TOKENS, TOP))
    gate_weight = jnp.clip(jnp.exp(math.log(1.0) - 2.9957323 * jax.random.uniform(key_of[3], (TOKENS, TOP), jnp.float32) ** levels(key_of[3], (TOKENS, TOP), ((0, 128),), -0.2, 0.2)), 0.05, 1.0)
    w_gate = gaussian(key_of[4], (EXPERTS, D, FF), D ** -0.5, 0.125, ((0, 32), (2, 8)))
    w_up = gaussian(key_of[5], (EXPERTS, D, FF), D ** -0.5, 0.125, ((0, 32), (2, 8)))
    w_down = gaussian(key_of[6], (EXPERTS, FF, D), FF ** -0.5, 0.15625, ((0, 32), (1, 8)))
    return {"tokens": tokens, "grad_mixed": grad_mixed, "expert_ids": expert_ids, "gate_weight": gate_weight, "w_gate": w_gate, "w_up": w_up, "w_down": w_down}


def slot_tables(expert_ids, gate_weight):
    blocks = expert_ids.shape[0] // TOK_DEV
    per_block = TOK_DEV * TOP
    flat = expert_ids.reshape(blocks, per_block)
    onehot = (flat[:, :, None] == jnp.arange(EXPERTS, dtype=jnp.int32)[None, None, :]).astype(jnp.int32)
    rank = jnp.sum((jnp.cumsum(onehot, axis=1) - onehot) * onehot, axis=2).astype(jnp.int32)
    block_ids = jnp.arange(blocks, dtype=jnp.int32)[:, None]
    group_of = jnp.broadcast_to(block_ids // N_HID, flat.shape).astype(jnp.int32)
    row_index = ((block_ids % N_HID) * CAP + rank).astype(jnp.int32)
    token_index = (jnp.arange(blocks * per_block, dtype=jnp.int32) // TOP).reshape(blocks, per_block)
    rows_group = N_HID * CAP
    token_of = jnp.zeros((EXPERTS, N_GROUP, rows_group), jnp.int32).at[flat, group_of, row_index].set(token_index)
    live_of = jnp.zeros((EXPERTS, N_GROUP, rows_group), jnp.float32).at[flat, group_of, row_index].set(1.0)
    gate_of = jnp.zeros((EXPERTS, N_GROUP, rows_group), jnp.float32).at[flat, group_of, row_index].set(
        gate_weight.reshape(blocks, per_block))
    return flat, group_of, row_index, token_of, live_of, gate_of


def group_terms(left, right):
    partial_value = jnp.einsum("gmp,gmq->gpq",
                         left.reshape(N_GROUP, -1, left.shape[1]).astype(jnp.float32),
                         right.reshape(N_GROUP, -1, right.shape[1]).astype(jnp.float32))
    partial_value = lax.optimization_barrier(partial_value.astype(jnp.bfloat16))
    return jnp.sum(partial_value.astype(jnp.float32), axis=0)


def reference(tokens, grad_mixed, expert_ids, gate_weight, w_gate, w_up, w_down):
    flat, group_of, row_index, token_of, live_of, gate_of = slot_tables(expert_ids, gate_weight)
    slice_width = FF // N_INGROUP
    width = tokens.shape[1]
    rows_all = N_GROUP * N_HID * CAP

    def expert(inputs):
        token_idx, live, gates, wgate, wup, wdown = inputs
        token_flat = token_idx.reshape(rows_all)
        live_flat = live.reshape(rows_all)
        gate_flat = gates.reshape(rows_all)
        x_rows = jnp.where(live_flat[:, None] > 0.5, tokens[token_flat], jnp.zeros((), jnp.bfloat16))
        gated = (gate_flat[:, None] * grad_mixed[token_flat].astype(jnp.float32)).astype(jnp.bfloat16)
        gate_pre = jnp.dot(x_rows, wgate, preferred_element_type=jnp.float32)
        up_pre = jnp.dot(x_rows, wup, preferred_element_type=jnp.float32)
        sigmoid_gate = jax.nn.sigmoid(gate_pre)
        silu = gate_pre * sigmoid_gate
        hidden = (silu * up_pre).astype(jnp.bfloat16)
        parts = jnp.einsum("mjh,jhd->jmd", hidden.reshape(rows_all, N_INGROUP, slice_width).astype(jnp.float32),
                           wdown.reshape(N_INGROUP, slice_width, width).astype(jnp.float32))
        parts = lax.optimization_barrier(parts.astype(jnp.bfloat16))
        out_rows = jnp.sum(parts.astype(jnp.float32), axis=0).astype(jnp.bfloat16)
        d_hidden = jnp.dot(gated, wdown.T, preferred_element_type=jnp.float32)
        d_up = (d_hidden * silu).astype(jnp.bfloat16)
        d_gate = (d_hidden * up_pre * sigmoid_gate * (1.0 + gate_pre * (1.0 - sigmoid_gate))).astype(jnp.bfloat16)
        g_down = group_terms(hidden, gated)
        g_gate = group_terms(x_rows, d_gate)
        g_up = group_terms(x_rows, d_up)
        back = jnp.einsum("mjh,djh->jmd", d_gate.reshape(rows_all, N_INGROUP, slice_width).astype(jnp.float32),
                          wgate.reshape(width, N_INGROUP, slice_width).astype(jnp.float32))
        back = back + jnp.einsum("mjh,djh->jmd", d_up.reshape(rows_all, N_INGROUP, slice_width).astype(jnp.float32),
                                 wup.reshape(width, N_INGROUP, slice_width).astype(jnp.float32))
        back = lax.optimization_barrier(back.astype(jnp.bfloat16))
        in_rows = jnp.sum(back.astype(jnp.float32), axis=0).astype(jnp.bfloat16)
        return out_rows, in_rows, g_gate, g_up, g_down

    out_rows, in_rows, grad_gate, grad_up, grad_down = lax.map(
        expert, (token_of, live_of, gate_of, w_gate, w_up, w_down))
    out_rows = out_rows.reshape(EXPERTS, N_GROUP, N_HID * CAP, width)
    in_rows = in_rows.reshape(EXPERTS, N_GROUP, N_HID * CAP, width)
    picked_out = out_rows[flat, group_of, row_index].reshape(tokens.shape[0], TOP, width)
    picked_in = in_rows[flat, group_of, row_index].reshape(tokens.shape[0], TOP, width)
    mixed = jnp.sum(gate_weight[:, :, None] * picked_out.astype(jnp.float32), axis=1).astype(jnp.bfloat16)
    grad_tokens = jnp.sum(picked_in.astype(jnp.float32), axis=1).astype(jnp.bfloat16)
    return mixed, grad_tokens, grad_gate, grad_up, grad_down
```

```python
import functools

import jax
import jax.numpy as jnp
from jax import lax
from jax.experimental import pallas as pl
from jax.experimental.pallas import tpu as pltpu
from jax.sharding import PartitionSpec as P

MESH = pl.DeviceIdType.MESH
BF = jnp.bfloat16
F32 = jnp.float32
CAP = 2
LANES = 128

NN = (((1,), (0,)), ((), ()))
NT = (((1,), (1,)), ((), ()))
TN = (((0,), (0,)), ((), ()))


def dot(a, b, dims=NN):
    return lax.dot_general(a, b, dims, preferred_element_type=F32)


def iota(shape, dim):
    return lax.broadcasted_iota(jnp.int32, shape, dim)


def kernel(
    dims,
    ids_ref, gw_ref, tok_hbm, grd_hbm, wg_hbm, wu_hbm, wd_hbm,
    mixed_ref, gtok_ref, gg_hbm, gu_hbm, gd_hbm,
    tok, grd, wg, wu, wd, sel, unperm, perm,
    tile_s, tile_r, acts, part_s, part_r, back_s, back_r,
    xg_r, hr, og, ou, od,
    in_sem, out_sem, send_sem, z_sem, y_sem, rs_sem, zb_sem, xg_sem, hr_sem,
):
    n_g, n_j, n_h, chunks, depth, per, top = dims
    rows = depth * CAP
    half = depth // 2
    toks = ids_ref.shape[0]
    g, j, h = lax.axis_index("group"), lax.axis_index("ingroup"), lax.axis_index("hid")
    width = 2 * LANES

    lanes = pl.ds(pl.multiple_of(j * width, width), width)
    loads = [
        pltpu.make_async_copy(src, dst, in_sem.at[n])
        for n, (src, dst) in enumerate(
            (
                (tok_hbm.at[:, lanes], tok),
                (grd_hbm.at[:, lanes], grd),
                (wg_hbm, wg),
                (wu_hbm, wu),
                (wd_hbm, wd),
            )
        )
    ]
    for load in loads:
        load.start()

    barrier = pltpu.get_barrier_semaphore()

    def greet(count, device):
        def body(o, carry):
            pl.semaphore_signal(
                barrier, inc=1, device_id=device(o), device_id_type=MESH
            )
            return carry

        lax.fori_loop(1, count, body, 0)

    def hid_peer(o):
        return (g, j, lax.rem(h + o, n_h))

    def in_peer(o):
        return (g, lax.rem(j + o, n_j), h)

    def group_peer(o):
        return (lax.rem(g + o, n_g), j, h)

    greet(n_h, hid_peer)
    greet(n_j, in_peer)
    greet(n_g, group_peer)

    total = n_h * 16
    lane = iota((1, total), 1)
    pos = lane // 16
    which, part = (lane // 8) % 2, (lane // 4) % 2
    expert_local, place = (lane // 2) % 2, lane % 2
    ck, i = pos // depth, pos % depth
    delta = jnp.where(
        i < half, n_h // 2 - half * (ck + 1) + i, n_h // 2 + half * ck + i - half
    )
    expert = ((h + delta) % n_h) * 2 + expert_local
    named = jnp.zeros((toks, total), F32)
    gates = jnp.zeros((toks, total), F32)
    for k in range(top):
        hit = (ids_ref[:, k : k + 1] == expert).astype(F32)
        named = named + hit
        gates = gates + hit * gw_ref[:, k : k + 1]
    earlier = (iota((toks, toks), 1) < iota((toks, toks), 0)).astype(BF)
    rank = dot(earlier, named.astype(BF))
    taken = named * (rank == place.astype(F32)).astype(F32)
    gates = gates * taken
    hi = gates.astype(BF)
    rest = gates - hi.astype(F32)
    mid = rest.astype(BF)
    lo = (rest - mid.astype(F32)).astype(BF)
    pick = taken.astype(BF)
    pieces = []
    for value, w in ((pick, 0), (hi, 1), (mid, 1), (lo, 1)):
        for p in range(2):
            pieces.append(value * ((which == w) & (part == p)).astype(BF))
    sel[...] = jnp.concatenate(pieces, axis=0)

    size = depth * 16

    def row_order(q):
        p, w = q // (size // 2), (q // (size // 4)) % 2
        e, t, c = (q // rows) % 2, (q // CAP) % depth, q % CAP
        return t * 16 + w * 8 + p * 4 + e * 2 + c

    unperm[...] = (row_order(iota((size, size), 0)) == iota((size, size), 1)).astype(BF)
    perm[...] = (row_order(iota((size, size), 1)) == iota((size, size), 0)).astype(BF)

    loads[0].wait()
    loads[1].wait()
    t0, t1 = tok[:, :LANES], tok[:, LANES:]
    g0, g1 = grd[:, :LANES], grd[:, LANES:]
    rhs = jnp.concatenate([t0, t1, g0, g1, g0, g1, g0, g1], axis=0)
    tile_s[...] = dot(sel[...], rhs, TN).astype(BF).reshape(n_h, 16, LANES)
    home = (chunks - 1) * depth
    tile_r[home] = tile_s[home]

    pl.semaphore_wait(barrier, n_h - 1 + n_j - 1 + n_g - 1)

    def distance(c, t):
        return jnp.where(
            t < half, n_h // 2 - half * (c + 1) + t, n_h // 2 + half * c + t - half
        )

    def z_send(c, src, dst, sign, send, recv):
        def body(t, carry):
            at = c * depth + t
            peer = lax.rem(h + n_h + sign * distance(c, t), n_h)
            pltpu.make_async_remote_copy(
                src.at[at], dst.at[at], send, recv, (g, j, peer), MESH
            ).start()
            return carry

        lax.fori_loop(1 if c == chunks - 1 else 0, depth, body, 0)

    def z_block(c, ref):
        return ref.at[pl.ds(c * depth + (c == chunks - 1), depth - (c == chunks - 1))]

    def wait_recv(ref, sem):
        pltpu.make_async_remote_copy(ref, ref, sem, sem, in_peer(1), MESH).wait_recv()

    def wait_send(ref, sem):
        pltpu.make_async_remote_copy(ref, ref, sem, sem, in_peer(1), MESH).wait_send()

    for c in range(chunks):
        z_send(c, tile_s, tile_r, 1, send_sem.at[0], z_sem.at[c])

    for c in range(chunks):
        wait_recv(z_block(c, tile_r), z_sem.at[c])
        tiles = tile_r[c * depth : (c + 1) * depth].reshape(size, LANES)
        ordered = dot(unperm[...], tiles).astype(BF)
        acts[j, c, :, :, :, :LANES] = ordered[: size // 2].reshape(2, 2, rows, LANES)
        acts[j, c, :, :, :, LANES:] = ordered[size // 2 :].reshape(2, 2, rows, LANES)

        def forward(o, carry, c=c):
            pltpu.make_async_remote_copy(
                acts.at[j, c], acts.at[j, c], send_sem.at[1], y_sem, in_peer(o), MESH
            ).start()
            return carry

        lax.fori_loop(1, n_j, forward, 0)
    for load in loads[2:]:
        load.wait()
    wait_recv(acts.at[pl.ds(0, n_j - 1)], y_sem)

    wide = n_j // n_g

    def rows_out(o, carry):
        there = lax.rem(g + o, n_g)
        pltpu.make_async_remote_copy(
            acts.at[pl.ds(there * wide, wide)], xg_r.at[g],
            send_sem.at[2], xg_sem, (there, j, h), MESH,
        ).start()
        return carry

    m = chunks * rows
    units = wg.shape[2]
    for e in range(2):
        gate_pre = jnp.zeros((m, units), F32)
        up_pre = jnp.zeros((m, units), F32)
        d_hidden = jnp.zeros((m, units), F32)
        for b in range(n_j):
            cols = slice(b * width, (b + 1) * width)
            x = acts[b, :, 0, e].reshape(m, width)
            gated = acts[b, :, 1, e].reshape(m, width)
            gate_pre = gate_pre + dot(x, wg[e, cols, :])
            up_pre = up_pre + dot(x, wu[e, cols, :])
            d_hidden = d_hidden + dot(gated, wd[e, :, cols], NT)
        sig = jax.nn.sigmoid(gate_pre)
        silu = gate_pre * sig
        hr[g, 0, e] = (silu * up_pre).astype(BF)
        d_gate = d_hidden * up_pre * sig * (1.0 + gate_pre * (1.0 - sig))
        hr[g, 1, e] = d_gate.astype(BF)
        hr[g, 2, e] = (d_hidden * silu).astype(BF)

    def hidden_out(o, carry):
        pltpu.make_async_remote_copy(
            hr.at[g], hr.at[g], send_sem.at[3], hr_sem, group_peer(o), MESH
        ).start()
        return carry

    def part_out(o, c):
        return pltpu.make_async_remote_copy(
            part_s.at[lax.rem(j + o, n_j), c], part_r.at[o - 1, c],
            send_sem.at[4], rs_sem.at[c], in_peer(o), MESH,
        )

    for e in range(2):
        hidden, d_gate, d_up = hr[g, 0, e], hr[g, 1, e], hr[g, 2, e]
        for b in range(n_j):
            cols = slice(b * width, (b + 1) * width)
            out = dot(hidden, wd[e, :, cols]).astype(BF)
            part_s[b, :, 1, e] = out.reshape(chunks, rows, width)
            back = dot(d_gate, wg[e, cols, :], NT) + dot(d_up, wu[e, cols, :], NT)
            part_s[b, :, 0, e] = back.astype(BF).reshape(chunks, rows, width)

    for c in range(chunks):

        def send_part(o, carry, c=c):
            part_out(o, c).start()
            return carry

        lax.fori_loop(1, n_j, send_part, 0)
    lax.fori_loop(1, n_g, hidden_out, 0)
    lax.fori_loop(1, n_g, rows_out, 0)

    for c in range(chunks):
        wait_recv(part_r.at[:, c], rs_sem.at[c])
        summed = part_s[j, c].astype(F32)
        for o in range(n_j - 1):
            summed = summed + part_r[o, c].astype(F32)
        summed = summed.astype(BF)
        both = jnp.concatenate(
            [
                summed[..., :LANES].reshape(size // 2, LANES),
                summed[..., LANES:].reshape(size // 2, LANES),
            ],
            axis=0,
        )
        tiles = dot(perm[...], both).astype(BF)
        back_s[c * depth : (c + 1) * depth] = tiles.reshape(depth, 16, LANES)
        z_send(c, back_s, back_r, -1, send_sem.at[5], zb_sem)
    back_r[home] = back_s[home]

    wait_recv(hr.at[pl.ds(0, n_g - 1)], hr_sem)
    wait_recv(xg_r.at[pl.ds(0, n_g - 1)], xg_sem)
    xg_r[g] = acts[pl.ds(g * wide, wide)]
    for e in range(2):
        ups = [hr[:, n, e].reshape(n_g * m, units) for n in range(3)]
        for b in range(wide):
            cols = slice(b * width, (b + 1) * width)
            x = xg_r[:, b, :, 0, e].reshape(n_g * m, width)
            gated = xg_r[:, b, :, 1, e].reshape(n_g * m, width)
            og[e, cols, :] = dot(x, ups[1], TN)
            ou[e, cols, :] = dot(x, ups[2], TN)
            od[e, :, cols] = dot(ups[0], gated, TN)
    stores = [
        pltpu.make_async_copy(src, dst, out_sem.at[n])
        for n, (src, dst) in enumerate(((og, gg_hbm), (ou, gu_hbm), (od, gd_hbm)))
    ]
    for store in stores:
        store.start()

    wait_recv(back_r.at[pl.ds(0, n_h - 1)], zb_sem)
    sums = dot(sel[...], back_r[...].reshape(total, LANES))
    at = [sums[n * toks : (n + 1) * toks] for n in range(8)]
    gtok_ref[:, :LANES] = at[0].astype(BF)
    gtok_ref[:, LANES:] = at[1].astype(BF)
    mixed_ref[:, :LANES] = (at[2] + at[4] + at[6]).astype(BF)
    mixed_ref[:, LANES:] = (at[3] + at[5] + at[7]).astype(BF)

    wait_send(tile_s.at[pl.ds(0, n_h - 1)], send_sem.at[0])
    wait_send(acts.at[pl.ds(0, n_j - 1)], send_sem.at[1])
    wait_send(xg_r.at[pl.ds(0, n_g - 1)], send_sem.at[2])
    wait_send(hr.at[pl.ds(0, n_g - 1)], send_sem.at[3])
    wait_send(part_r, send_sem.at[4])
    wait_send(back_s.at[pl.ds(0, n_h - 1)], send_sem.at[5])
    for store in stores:
        store.wait()


def layer(tokens, grad_mixed, expert_ids, gate_weight, w_gate, w_up, w_down):
    n_g, n_j, n_h = (lax.axis_size(a) for a in ("group", "ingroup", "hid"))
    per, d_model, units = w_gate.shape
    toks, top = expert_ids.shape
    depth = min(8, n_h // 2)
    chunks = n_h // depth
    rows = depth * CAP
    width = 2 * LANES
    wide = n_j // n_g
    m = chunks * rows
    share = d_model // n_g
    vmem, hbm = pl.BlockSpec(memory_space=pltpu.VMEM), pl.BlockSpec(memory_space=pl.ANY)
    block = (chunks, 2, per, rows, width)
    dma = pltpu.SemaphoreType.DMA
    return pl.pallas_call(
        functools.partial(kernel, (n_g, n_j, n_h, chunks, depth, per, top)),
        out_shape=(
            jax.ShapeDtypeStruct((toks, width), BF),
            jax.ShapeDtypeStruct((toks, width), BF),
            jax.ShapeDtypeStruct((per, share, units), F32),
            jax.ShapeDtypeStruct((per, share, units), F32),
            jax.ShapeDtypeStruct((per, units, share), F32),
        ),
        in_specs=[vmem] * 2 + [hbm] * 5,
        out_specs=(vmem, vmem, hbm, hbm, hbm),
        scratch_shapes=[
            pltpu.VMEM((toks, width), BF),
            pltpu.VMEM((toks, width), BF),
            pltpu.VMEM(w_gate.shape, BF),
            pltpu.VMEM(w_up.shape, BF),
            pltpu.VMEM(w_down.shape, BF),
            pltpu.VMEM((8 * toks, n_h * 16), BF),
            pltpu.VMEM((depth * 16, depth * 16), BF),
            pltpu.VMEM((depth * 16, depth * 16), BF),
            pltpu.VMEM((n_h, 16, LANES), BF),
            pltpu.VMEM((n_h, 16, LANES), BF),
            pltpu.VMEM((n_j, *block), BF),
            pltpu.VMEM((n_j, *block), BF),
            pltpu.VMEM((n_j - 1, *block), BF),
            pltpu.VMEM((n_h, 16, LANES), BF),
            pltpu.VMEM((n_h, 16, LANES), BF),
            pltpu.VMEM((n_g, wide, *block), BF),
            pltpu.VMEM((n_g, 3, per, m, units), BF),
            pltpu.VMEM((per, share, units), F32),
            pltpu.VMEM((per, share, units), F32),
            pltpu.VMEM((per, units, share), F32),
            dma((5,)),
            dma((3,)),
            dma((6,)),
            dma((chunks,)),
            dma,
            dma((chunks,)),
            dma,
            dma,
            dma,
        ],
        compiler_params=pltpu.CompilerParams(
            collective_id=0, has_side_effects=True, vmem_limit_bytes=48 * 2**20
        ),
    )(expert_ids, gate_weight, tokens, grad_mixed, w_gate, w_up, w_down)


def solution(mesh):
    both = P(("group", "hid"), None)
    return jax.shard_map(
        layer,
        mesh=mesh,
        in_specs=(
            both,
            both,
            both,
            both,
            P("hid", None, "ingroup"),
            P("hid", None, "ingroup"),
            P("hid", "ingroup", None),
        ),
        out_specs=(
            P(("group", "hid"), "ingroup"),
            P(("group", "hid"), "ingroup"),
            P("hid", "group", "ingroup"),
            P("hid", "group", "ingroup"),
            P("hid", "ingroup", "group"),
        ),
        check_vma=False,
    )
```

```python
import functools

import jax
import jax.numpy as jnp
from jax import lax
from jax.experimental import pallas as pl
from jax.experimental.pallas import tpu as pltpu
from jax.sharding import PartitionSpec as P

MESH = pl.DeviceIdType.MESH
BF = jnp.bfloat16
F32 = jnp.float32
CAP = 2
LANES = 128

NN = (((1,), (0,)), ((), ()))
NT = (((1,), (1,)), ((), ()))
TN = (((0,), (0,)), ((), ()))


def dot(a, b, dims=NN):
    return lax.dot_general(a, b, dims, preferred_element_type=F32)


def iota(shape, dim):
    return lax.broadcasted_iota(jnp.int32, shape, dim)


def kernel(
    dims,
    ids_hbm, gw_hbm, tok_hbm, grd_hbm, wg_hbm, wu_hbm, wd_hbm,
    mixed_hbm, gtok_hbm, gg_hbm, gu_hbm, gd_hbm,
    ids, gw, tok, grd, wg, wu, wd, sel, unperm, perm,
    tile_s, tile_r, acts, part_s, twin_r, pair_s, part_r, back_s, back_r,
    xg_r, hr, mixed, gtok, og, ou, od,
    in_sem, out_sem, send_sem, z_sem, y_sem, twin_sem, pair_sem, rs_sem, zb_sem, xg_sem, hr_sem,
):
    n_g, n_j, n_h, chunks, depth, per, top = dims
    rows = depth * CAP
    half = depth // 2
    toks = ids_hbm.shape[1]
    g, j, h = lax.axis_index("group"), lax.axis_index("ingroup"), lax.axis_index("hid")
    width = 2 * LANES

    lanes = pl.ds(pl.multiple_of(j * width, width), width)
    loads = [
        pltpu.make_async_copy(src, dst, in_sem.at[n])
        for n, (src, dst) in enumerate(
            (
                (ids_hbm, ids),
                (gw_hbm, gw),
                (tok_hbm.at[:, lanes], tok),
                (grd_hbm.at[:, lanes], grd),
                (wg_hbm, wg),
                (wu_hbm, wu),
                (wd_hbm, wd),
            )
        )
    ]
    for load in loads:
        load.start()
    sent = []

    barrier = pltpu.get_barrier_semaphore()

    def greet(count, device):
        def body(o, carry):
            pl.semaphore_signal(
                barrier, inc=1, device_id=device(o), device_id_type=MESH
            )
            return carry

        lax.fori_loop(1, count, body, 0)

    def hid_peer(o):
        return (g, j, lax.rem(h + o, n_h))

    n_y, y, core = n_j // 2, j // 2, j % 2
    twin = (g, 2 * y + 1 - core, h)

    def y_at(o):
        return lax.rem(y + o, n_y)

    def y_peer(o):
        return (g, 2 * y_at(o) + core, h)

    def group_peer(o):
        return (lax.rem(g + o, n_g), j, h)

    greet(n_h, hid_peer)
    greet(n_y, y_peer)
    pl.semaphore_signal(barrier, inc=1, device_id=twin, device_id_type=MESH)
    greet(n_g, group_peer)

    total = n_h * 16
    lane = iota((1, total), 1)
    pos = lane // 16
    which, part = (lane // 8) % 2, (lane // 4) % 2
    expert_local, place = (lane // 2) % 2, lane % 2
    ck, i = pos // depth, pos % depth
    delta = jnp.where(
        i < half, n_h // 2 - half * (ck + 1) + i, n_h // 2 + half * ck + i - half
    )
    expert = ((h + delta) % n_h) * 2 + expert_local
    named = jnp.zeros((toks, total), F32)
    gates = jnp.zeros((toks, total), F32)
    loads[0].wait()
    loads[1].wait()
    same = iota((toks, toks), 0) == iota((toks, toks), 1)

    def column(row):
        return jnp.sum(jnp.where(same, row.astype(F32), 0.0), axis=1, keepdims=True)

    wanted = expert.astype(F32)
    for k in range(top):
        hit = (column(ids[k : k + 1, :]) == wanted).astype(F32)
        named = named + hit
        gates = gates + hit * column(gw[k : k + 1, :])
    earlier = (iota((toks, toks), 1) < iota((toks, toks), 0)).astype(BF)
    rank = dot(earlier, named.astype(BF))
    taken = named * (rank == place.astype(F32)).astype(F32)
    gates = gates * taken
    hi = gates.astype(BF)
    rest = gates - hi.astype(F32)
    mid = rest.astype(BF)
    lo = (rest - mid.astype(F32)).astype(BF)
    pick = taken.astype(BF)
    pieces = []
    for value, w in ((pick, 0), (hi, 1), (mid, 1), (lo, 1)):
        for p in range(2):
            pieces.append(value * ((which == w) & (part == p)).astype(BF))
    sel[...] = jnp.concatenate(pieces, axis=0)

    size = depth * 16

    def row_order(q):
        p, w = q // (size // 2), (q // (size // 4)) % 2
        e, t, c = (q // rows) % 2, (q // CAP) % depth, q % CAP
        return t * 16 + w * 8 + p * 4 + e * 2 + c

    unperm[...] = (row_order(iota((size, size), 0)) == iota((size, size), 1)).astype(BF)
    perm[...] = (row_order(iota((size, size), 1)) == iota((size, size), 0)).astype(BF)

    loads[2].wait()
    loads[3].wait()
    t0, t1 = tok[:, :LANES], tok[:, LANES:]
    g0, g1 = grd[:, :LANES], grd[:, LANES:]
    rhs = jnp.concatenate([t0, t1, g0, g1, g0, g1, g0, g1], axis=0)
    tile_s[...] = dot(sel[...], rhs, TN).astype(BF).reshape(n_h, 16, LANES)
    home = (chunks - 1) * depth
    tile_r[home] = tile_s[home]

    pl.semaphore_wait(barrier, n_h - 1 + n_y - 1 + 1 + n_g - 1)

    def wait_recv(ref, sem):
        pltpu.make_async_remote_copy(ref, ref, sem, sem, twin, MESH).wait_recv()

    def wait_send(ref, sem):
        pltpu.make_async_remote_copy(ref, ref, sem, sem, twin, MESH).wait_send()

    def distance(c, t):
        return jnp.where(
            t < half, n_h // 2 - half * (c + 1) + t, n_h // 2 + half * c + t - half
        )

    def z_send(c, src, dst, sign, send, recv):
        def body(t, carry):
            t = jnp.where(t % 2 == 0, t // 2, depth - 1 - t // 2)
            at = c * depth + t
            peer = lax.rem(h + n_h + sign * distance(c, t), n_h)
            pltpu.make_async_remote_copy(
                src.at[at], dst.at[at], send, recv, (g, j, peer), MESH
            ).start()
            return carry

        lax.fori_loop(1 if c == chunks - 1 else 0, depth, body, 0)

    def z_block(c, ref):
        return ref.at[pl.ds(c * depth + (c == chunks - 1), depth - (c == chunks - 1))]

    last = chunks - 1
    order = [*range(last - 1), last, last - 1]
    for c in order:
        z_send(c, tile_s, tile_r, 1, send_sem.at[0], z_sem.at[c])
    sent.append((tile_s.at[pl.ds(0, n_h - 1)], send_sem.at[0]))

    def to_twin(b, c):
        pltpu.make_async_remote_copy(
            acts.at[b, c], acts.at[b, c], send_sem.at[6], twin_sem, twin, MESH
        ).start()

    def pass_on(c):
        wait_recv(acts.at[pl.ds(0, n_y - 1), c], y_sem.at[c])

        def body(o, carry):
            to_twin(2 * y_at(o) + core, c)
            return carry

        lax.fori_loop(1, n_y, body, 0)

    before = None
    for c in (last, *range(last)):
        wait_recv(z_block(c, tile_r), z_sem.at[c])
        tiles = tile_r[c * depth : (c + 1) * depth].reshape(size, LANES)
        ordered = dot(unperm[...], tiles).astype(BF)
        acts[j, c, :, :, :, :LANES] = ordered[: size // 2].reshape(2, 2, rows, LANES)
        acts[j, c, :, :, :, LANES:] = ordered[size // 2 :].reshape(2, 2, rows, LANES)

        def forward(o, carry, c=c):
            pltpu.make_async_remote_copy(
                acts.at[j, c], acts.at[j, c],
                send_sem.at[1], y_sem.at[c], y_peer(o), MESH,
            ).start()
            return carry

        lax.fori_loop(1, n_y, forward, 0)
        to_twin(j, c)
        if before is not None:
            pass_on(before)
        before = c
    pass_on(before)
    sent.append((acts.at[pl.ds(0, n_y - 1)], send_sem.at[1]))
    sent.append((acts.at[pl.ds(0, n_y)], send_sem.at[6]))
    for load in loads[4:]:
        load.wait()
    wait_recv(acts.at[pl.ds(0, n_y)], twin_sem)

    wide = n_j // n_g

    def rows_out(o, carry):
        there = lax.rem(g + o, n_g)
        pltpu.make_async_remote_copy(
            acts.at[pl.ds(there * wide, wide)], xg_r.at[g],
            send_sem.at[2], xg_sem, (there, j, h), MESH,
        ).start()
        return carry

    lax.fori_loop(1, n_g, rows_out, 0)
    sent.append((xg_r.at[pl.ds(0, n_g - 1)], send_sem.at[2]))

    m = chunks * rows
    units = wg.shape[1]
    hiddens = []
    for e in range(2):
        gate_pre = jnp.zeros((m, units), F32)
        up_pre = jnp.zeros((m, units), F32)
        d_hidden = jnp.zeros((m, units), F32)
        for b in range(n_j):
            cols = slice(b * width, (b + 1) * width)
            x = acts[b, :, 0, e].reshape(m, width)
            gated = acts[b, :, 1, e].reshape(m, width)
            gate_pre = gate_pre + dot(x, wg[e, :, cols], NT)
            up_pre = up_pre + dot(x, wu[e, :, cols], NT)
            d_hidden = d_hidden + dot(gated, wd[e, :, cols], NT)
        sig = jax.nn.sigmoid(gate_pre)
        silu = gate_pre * sig
        d_gate = d_hidden * up_pre * sig * (1.0 + gate_pre * (1.0 - sig))
        hiddens.append(
            [v.astype(BF) for v in (silu * up_pre, d_gate, d_hidden * silu)]
        )
    for n in range(3):
        hr[g, n] = jnp.concatenate([hiddens[0][n], hiddens[1][n]], axis=1)

    def hidden_out(o, carry):
        pltpu.make_async_remote_copy(
            hr.at[g], hr.at[g], send_sem.at[3], hr_sem, group_peer(o), MESH
        ).start()
        return carry

    lax.fori_loop(1, n_g, hidden_out, 0)
    sent.append((hr.at[pl.ds(0, n_g - 1)], send_sem.at[3]))

    for e in range(2):
        hidden, d_gate, d_up = hiddens[e]
        for b in range(n_j):
            cols = slice(b * width, (b + 1) * width)
            out = dot(hidden, wd[e, :, cols]).astype(BF)
            part_s[b, :, 1, e] = out.reshape(chunks, rows, width)
            back = dot(d_gate, wg[e, :, cols]) + dot(d_up, wu[e, :, cols])
            part_s[b, :, 0, e] = back.astype(BF).reshape(chunks, rows, width)

    for c in range(chunks):

        def twin_part(b, carry, c=c):
            pltpu.make_async_remote_copy(
                part_s.at[2 * b + 1 - core, c], twin_r.at[b, c],
                send_sem.at[7], pair_sem.at[c], twin, MESH,
            ).start()
            return carry

        lax.fori_loop(0, n_y, twin_part, 0)
    sent.append((twin_r, send_sem.at[7]))

    def pair(c):
        wait_recv(twin_r.at[:, c], pair_sem.at[c])

        def body(o, carry):
            there = y_at(o)
            mine = part_s[2 * there + core, c].astype(F32)
            pair_s[there, c] = (mine + twin_r[there, c].astype(F32)).astype(BF)
            pltpu.make_async_remote_copy(
                pair_s.at[there, c], part_r.at[o - 1, c],
                send_sem.at[4], rs_sem.at[c], y_peer(o), MESH,
            ).start()
            return carry

        lax.fori_loop(1, n_y, body, 0)

    for c in range(chunks):
        if c == 0:
            pair(0)
        if c + 1 < chunks:
            pair(c + 1)
        summed = part_s[j, c].astype(F32) + twin_r[y, c].astype(F32)
        wait_recv(part_r.at[:, c], rs_sem.at[c])
        for o in range(n_y - 1):
            summed = summed + part_r[o, c].astype(F32)
        summed = summed.astype(BF)
        both = jnp.concatenate(
            [
                summed[..., :LANES].reshape(size // 2, LANES),
                summed[..., LANES:].reshape(size // 2, LANES),
            ],
            axis=0,
        )
        tiles = dot(perm[...], both).astype(BF)
        back_s[c * depth : (c + 1) * depth] = tiles.reshape(depth, 16, LANES)
        z_send(c, back_s, back_r, -1, send_sem.at[5], zb_sem)
    sent.append((part_r, send_sem.at[4]))
    sent.append((back_s.at[pl.ds(0, n_h - 1)], send_sem.at[5]))
    back_r[home] = back_s[home]

    wait_recv(hr.at[pl.ds(0, n_g - 1)], hr_sem)
    wait_recv(xg_r.at[pl.ds(0, n_g - 1)], xg_sem)
    xg_r[g] = acts[pl.ds(g * wide, wide)]
    for e in range(2):
        mine = slice(e * units, (e + 1) * units)
        ups = [hr[:, n, :, mine].reshape(n_g * m, units) for n in range(3)]
        for b in range(wide):
            cols = slice(b * width, (b + 1) * width)
            x = xg_r[:, b, :, 0, e].reshape(n_g * m, width)
            gated = xg_r[:, b, :, 1, e].reshape(n_g * m, width)
            og[e, :, cols] = dot(ups[1], x, TN)
            ou[e, :, cols] = dot(ups[2], x, TN)
            od[e, :, cols] = dot(ups[0], gated, TN)
    stores = [
        pltpu.make_async_copy(src, dst, out_sem.at[n])
        for n, (src, dst) in enumerate(
            (
                (og, gg_hbm),
                (ou, gu_hbm),
                (od, gd_hbm),
                (mixed, mixed_hbm),
                (gtok, gtok_hbm),
            )
        )
    ]
    for store in stores[:3]:
        store.start()

    wait_recv(back_r.at[pl.ds(0, n_h - 1)], zb_sem)
    sums = dot(sel[...], back_r[...].reshape(total, LANES))
    at = [sums[n * toks : (n + 1) * toks] for n in range(8)]
    gtok[:, :LANES] = at[0].astype(BF)
    gtok[:, LANES:] = at[1].astype(BF)
    mixed[:, :LANES] = (at[2] + at[4] + at[6]).astype(BF)
    mixed[:, LANES:] = (at[3] + at[5] + at[7]).astype(BF)

    for store in stores[3:]:
        store.start()

    for ref, sem in sent:
        wait_send(ref, sem)
    for store in stores:
        store.wait()


def hand_over(a, b, c, d, e, ao, bo, co, do, eo, av, bv, cv, dv, ev, get_sem, put_sem):
    gets, puts = [], []
    for n, (src, held, dst) in enumerate(
        ((a, av, ao), (b, bv, bo), (c, cv, co), (d, dv, do), (e, ev, eo))
    ):
        gets.append(pltpu.make_async_copy(src, held, get_sem.at[n]))
        puts.append(pltpu.make_async_copy(held, dst, put_sem.at[n]))
    for get in gets:
        get.start()
    for get, put in zip(gets, puts, strict=True):
        get.wait()
        put.start()
    for put in puts:
        put.wait()


def layer(tokens, grad_mixed, expert_ids, gate_weight, w_gate, w_up, w_down):
    expert_ids, gate_weight = expert_ids.T, gate_weight.T
    w_gate, w_up = jnp.swapaxes(w_gate, 1, 2), jnp.swapaxes(w_up, 1, 2)
    n_g, n_j, n_h = (lax.axis_size(a) for a in ("group", "ingroup", "hid"))
    per, units, d_model = w_gate.shape
    top, toks = expert_ids.shape
    depth = min(8, n_h // 2)
    chunks = n_h // depth
    rows = depth * CAP
    width = 2 * LANES
    wide = n_j // n_g
    m = chunks * rows
    share = d_model // n_g
    hbm = pl.BlockSpec(memory_space=pl.ANY)
    block = (chunks, 2, per, rows, width)
    dma = pltpu.SemaphoreType.DMA
    outs = pl.pallas_call(
        functools.partial(kernel, (n_g, n_j, n_h, chunks, depth, per, top)),
        out_shape=(
            jax.ShapeDtypeStruct((toks, width), BF),
            jax.ShapeDtypeStruct((toks, width), BF),
            jax.ShapeDtypeStruct((per, units, share), F32),
            jax.ShapeDtypeStruct((per, units, share), F32),
            jax.ShapeDtypeStruct((per, units, share), F32),
        ),
        in_specs=[hbm] * 7,
        out_specs=(hbm,) * 5,
        scratch_shapes=[
            pltpu.VMEM((top, toks), jnp.int32),
            pltpu.VMEM((top, toks), F32),
            pltpu.VMEM((toks, width), BF),
            pltpu.VMEM((toks, width), BF),
            pltpu.VMEM(w_gate.shape, BF),
            pltpu.VMEM(w_up.shape, BF),
            pltpu.VMEM(w_down.shape, BF),
            pltpu.VMEM((8 * toks, n_h * 16), BF),
            pltpu.VMEM((depth * 16, depth * 16), BF),
            pltpu.VMEM((depth * 16, depth * 16), BF),
            pltpu.VMEM((n_h, 16, LANES), BF),
            pltpu.VMEM((n_h, 16, LANES), BF),
            pltpu.VMEM((n_j, *block), BF),
            pltpu.VMEM((n_j, *block), BF),
            pltpu.VMEM((n_j // 2, *block), BF),
            pltpu.VMEM((n_j // 2, *block), BF),
            pltpu.VMEM((n_j // 2 - 1, *block), BF),
            pltpu.VMEM((n_h, 16, LANES), BF),
            pltpu.VMEM((n_h, 16, LANES), BF),
            pltpu.VMEM((n_g, wide, *block), BF),
            pltpu.VMEM((n_g, 3, m, per * units), BF),
            pltpu.VMEM((toks, width), BF),
            pltpu.VMEM((toks, width), BF),
            pltpu.VMEM((per, units, share), F32),
            pltpu.VMEM((per, units, share), F32),
            pltpu.VMEM((per, units, share), F32),
            dma((7,)),
            dma((5,)),
            dma((8,)),
            dma((chunks,)),
            dma((chunks,)),
            dma,
            dma((chunks,)),
            dma((chunks,)),
            dma,
            dma,
            dma,
        ],
        compiler_params=pltpu.CompilerParams(
            collective_id=0, has_side_effects=True, vmem_limit_bytes=60 * 2**20
        ),
    )(expert_ids, gate_weight, tokens, grad_mixed, w_gate, w_up, w_down)
    mixed, gtok, gg, gu, gd = pl.pallas_call(
        hand_over,
        out_shape=tuple(jax.ShapeDtypeStruct(o.shape, o.dtype) for o in outs),
        in_specs=[hbm] * 5,
        out_specs=(hbm,) * 5,
        scratch_shapes=[*(pltpu.VMEM(o.shape, o.dtype) for o in outs), dma((5,)), dma((5,))],
    )(*outs)
    return mixed, gtok, jnp.swapaxes(gg, 1, 2), jnp.swapaxes(gu, 1, 2), gd


def solution(mesh):
    both = P(("group", "hid"), None)
    return jax.shard_map(
        layer,
        mesh=mesh,
        in_specs=(
            both,
            both,
            both,
            both,
            P("hid", None, "ingroup"),
            P("hid", None, "ingroup"),
            P("hid", "ingroup", None),
        ),
        out_specs=(
            P(("group", "hid"), "ingroup"),
            P(("group", "hid"), "ingroup"),
            P("hid", "group", "ingroup"),
            P("hid", "group", "ingroup"),
            P("hid", "ingroup", "group"),
        ),
        check_vma=False,
    )
```

```python
import functools

import jax
import jax.numpy as jnp
from jax import lax
from jax.experimental import pallas as pl
from jax.experimental.pallas import tpu as pltpu
from jax.sharding import PartitionSpec as P

MESH = pl.DeviceIdType.MESH
BF = jnp.bfloat16
F32 = jnp.float32
CAP = 2
LANES = 128

NN = (((1,), (0,)), ((), ()))
NT = (((1,), (1,)), ((), ()))
TN = (((0,), (0,)), ((), ()))


def dot(a, b, dims=NN):
    return lax.dot_general(a, b, dims, preferred_element_type=F32)


def iota(shape, dim):
    return lax.broadcasted_iota(jnp.int32, shape, dim)


def kernel(
    dims,
    ids_hbm, gw_hbm, tok_hbm, grd_hbm, wg_hbm, wu_hbm, wd_hbm,
    mixed_hbm, gtok_hbm, gg_hbm, gu_hbm, gd_hbm,
    ids, gw, tok, grd, wg, wu, wd, sel, unperm, perm,
    tile_s, tile_r, acts, part_s, twin_r, pair_s, part_r, back_s, back_r,
    xg_r, hr, mixed, gtok, og, ou, od,
    in_sem, out_sem, send_sem, z_sem, y_sem, twin_sem, pair_sem, rs_sem, zb_sem, xg_sem, xt_sem, hr_sem,
):
    n_g, n_j, n_h, chunks, depth, per, top = dims
    rows = depth * CAP
    half = depth // 2
    toks = ids_hbm.shape[1]
    g, j, h = lax.axis_index("group"), lax.axis_index("ingroup"), lax.axis_index("hid")
    width = 2 * LANES

    lanes = pl.ds(pl.multiple_of(j * width, width), width)
    loads = [
        pltpu.make_async_copy(src, dst, in_sem.at[n])
        for n, (src, dst) in enumerate(
            (
                (ids_hbm, ids),
                (gw_hbm, gw),
                (tok_hbm.at[:, lanes], tok),
                (grd_hbm.at[:, lanes], grd),
                (wg_hbm, wg),
                (wu_hbm, wu),
                (wd_hbm, wd),
            )
        )
    ]
    for load in loads:
        load.start()
    sent = []

    barrier = pltpu.get_barrier_semaphore()

    def greet(count, device):
        def body(o, carry):
            pl.semaphore_signal(
                barrier, inc=1, device_id=device(o), device_id_type=MESH
            )
            return carry

        lax.fori_loop(1, count, body, 0)

    def hid_peer(o):
        return (g, j, lax.rem(h + o, n_h))

    n_y, y, core = n_j // 2, j // 2, j % 2
    twin = (g, 2 * y + 1 - core, h)

    def y_at(o):
        return lax.rem(y + o, n_y)

    def y_peer(o):
        return (g, 2 * y_at(o) + core, h)

    def group_peer(o):
        return (lax.rem(g + o, n_g), j, h)

    greet(n_h, hid_peer)
    greet(n_y, y_peer)
    pl.semaphore_signal(barrier, inc=1, device_id=twin, device_id_type=MESH)
    greet(n_g, group_peer)

    total = n_h * 16
    lane = iota((1, total), 1)
    pos = lane // 16
    which, part = (lane // 8) % 2, (lane // 4) % 2
    expert_local, place = (lane // 2) % 2, lane % 2
    ck, i = pos // depth, pos % depth
    delta = jnp.where(
        i < half, n_h // 2 - half * (ck + 1) + i, n_h // 2 + half * ck + i - half
    )
    expert = ((h + delta) % n_h) * 2 + expert_local
    named = jnp.zeros((toks, total), F32)
    gates = jnp.zeros((toks, total), F32)
    loads[0].wait()
    loads[1].wait()
    same = iota((toks, toks), 0) == iota((toks, toks), 1)

    def column(row):
        return jnp.sum(jnp.where(same, row.astype(F32), 0.0), axis=1, keepdims=True)

    wanted = expert.astype(F32)
    for k in range(top):
        hit = (column(ids[k : k + 1, :]) == wanted).astype(F32)
        named = named + hit
        gates = gates + hit * column(gw[k : k + 1, :])
    earlier = (iota((toks, toks), 1) < iota((toks, toks), 0)).astype(BF)
    rank = dot(earlier, named.astype(BF))
    taken = named * (rank == place.astype(F32)).astype(F32)
    gates = gates * taken
    hi = gates.astype(BF)
    rest = gates - hi.astype(F32)
    mid = rest.astype(BF)
    lo = (rest - mid.astype(F32)).astype(BF)
    pick = taken.astype(BF)
    pieces = []
    for value, w in ((pick, 0), (hi, 1), (mid, 1), (lo, 1)):
        for p in range(2):
            pieces.append(value * ((which == w) & (part == p)).astype(BF))
    sel[...] = jnp.concatenate(pieces, axis=0)

    size = depth * 16

    def row_order(q):
        p, w = q // (size // 2), (q // (size // 4)) % 2
        e, t, c = (q // rows) % 2, (q // CAP) % depth, q % CAP
        return t * 16 + w * 8 + p * 4 + e * 2 + c

    unperm[...] = (row_order(iota((size, size), 0)) == iota((size, size), 1)).astype(BF)
    perm[...] = (row_order(iota((size, size), 1)) == iota((size, size), 0)).astype(BF)

    loads[2].wait()
    loads[3].wait()
    t0, t1 = tok[:, :LANES], tok[:, LANES:]
    g0, g1 = grd[:, :LANES], grd[:, LANES:]
    rhs = jnp.concatenate([t0, t1, g0, g1, g0, g1, g0, g1], axis=0)
    tile_s[...] = dot(sel[...], rhs, TN).astype(BF).reshape(n_h, 16, LANES)
    home = (chunks - 1) * depth
    tile_r[home] = tile_s[home]

    pl.semaphore_wait(barrier, n_h - 1 + n_y - 1 + 1 + n_g - 1)

    def wait_recv(ref, sem):
        pltpu.make_async_remote_copy(ref, ref, sem, sem, twin, MESH).wait_recv()

    def wait_send(ref, sem):
        pltpu.make_async_remote_copy(ref, ref, sem, sem, twin, MESH).wait_send()

    def distance(c, t):
        return jnp.where(
            t < half, n_h // 2 - half * (c + 1) + t, n_h // 2 + half * c + t - half
        )

    def z_send(c, src, dst, sign, send, recv):
        def body(t, carry):
            t = jnp.where(t % 2 == 0, t // 2, depth - 1 - t // 2)
            at = c * depth + t
            peer = lax.rem(h + n_h + sign * distance(c, t), n_h)
            pltpu.make_async_remote_copy(
                src.at[at], dst.at[at], send, recv, (g, j, peer), MESH
            ).start()
            return carry

        lax.fori_loop(1 if c == chunks - 1 else 0, depth, body, 0)

    def z_block(c, ref):
        return ref.at[pl.ds(c * depth + (c == chunks - 1), depth - (c == chunks - 1))]

    last = chunks - 1
    order = [*range(last - 1), last, last - 1]
    for c in order:
        z_send(c, tile_s, tile_r, 1, send_sem.at[0], z_sem.at[c])
    sent.append((tile_s.at[pl.ds(0, n_h - 1)], send_sem.at[0]))

    def to_twin(b, c):
        pltpu.make_async_remote_copy(
            acts.at[b, c], acts.at[b, c], send_sem.at[6], twin_sem, twin, MESH
        ).start()

    def pass_on(c):
        wait_recv(acts.at[pl.ds(0, n_y - 1), c], y_sem.at[c])

        def body(o, carry):
            to_twin(2 * y_at(o) + core, c)
            return carry

        lax.fori_loop(1, n_y, body, 0)

    for c in (last, *range(last)):
        wait_recv(z_block(c, tile_r), z_sem.at[c])
        tiles = tile_r[c * depth : (c + 1) * depth].reshape(size, LANES)
        ordered = dot(unperm[...], tiles).astype(BF)
        acts[j, c, :, :, :, :LANES] = ordered[: size // 2].reshape(2, 2, rows, LANES)
        acts[j, c, :, :, :, LANES:] = ordered[size // 2 :].reshape(2, 2, rows, LANES)

        def forward(o, carry, c=c):
            pltpu.make_async_remote_copy(
                acts.at[j, c], acts.at[j, c],
                send_sem.at[1], y_sem.at[c], y_peer(o), MESH,
            ).start()
            return carry

        lax.fori_loop(1, n_y, forward, 0)
        to_twin(j, c)
    for c in (last, *range(last)):
        pass_on(c)
    sent.append((acts.at[pl.ds(0, n_y - 1)], send_sem.at[1]))
    sent.append((acts.at[pl.ds(0, n_y)], send_sem.at[6]))
    for load in loads[4:]:
        load.wait()
    wait_recv(acts.at[pl.ds(0, n_y)], twin_sem)


    def rows_out(o, carry):
        there = lax.rem(g + o, n_g)
        pltpu.make_async_remote_copy(
            acts.at[2 * there + core], xg_r.at[g, core],
            send_sem.at[2], xg_sem, (there, j, h), MESH,
        ).start()
        return carry

    lax.fori_loop(1, n_g, rows_out, 0)
    sent.append((xg_r.at[pl.ds(0, n_g - 1), 0], send_sem.at[2]))

    m = chunks * rows
    units = wg.shape[1]
    hiddens = []
    for e in range(2):
        gate_pre = jnp.zeros((m, units), F32)
        up_pre = jnp.zeros((m, units), F32)
        d_hidden = jnp.zeros((m, units), F32)
        for b in range(n_j):
            cols = slice(b * width, (b + 1) * width)
            x = acts[b, :, 0, e].reshape(m, width)
            gated = acts[b, :, 1, e].reshape(m, width)
            gate_pre = gate_pre + dot(x, wg[e, :, cols], NT)
            up_pre = up_pre + dot(x, wu[e, :, cols], NT)
            d_hidden = d_hidden + dot(gated, wd[e, :, cols], NT)
        sig = jax.nn.sigmoid(gate_pre)
        silu = gate_pre * sig
        d_gate = d_hidden * up_pre * sig * (1.0 + gate_pre * (1.0 - sig))
        hiddens.append(
            [v.astype(BF) for v in (silu * up_pre, d_gate, d_hidden * silu)]
        )
    for n in range(3):
        hr[g, n] = jnp.concatenate([hiddens[0][n], hiddens[1][n]], axis=1)

    def hidden_out(o, carry):
        pltpu.make_async_remote_copy(
            hr.at[g], hr.at[g], send_sem.at[3], hr_sem, group_peer(o), MESH
        ).start()
        return carry

    lax.fori_loop(1, n_g, hidden_out, 0)
    sent.append((hr.at[pl.ds(0, n_g - 1)], send_sem.at[3]))

    for e in range(2):
        hidden, d_gate, d_up = hiddens[e]
        for b in range(n_j):
            cols = slice(b * width, (b + 1) * width)
            out = dot(hidden, wd[e, :, cols]).astype(BF)
            part_s[b, :, 1, e] = out.reshape(chunks, rows, width)
            back = dot(d_gate, wg[e, :, cols]) + dot(d_up, wu[e, :, cols])
            part_s[b, :, 0, e] = back.astype(BF).reshape(chunks, rows, width)

    for c in range(chunks):

        def twin_part(b, carry, c=c):
            pltpu.make_async_remote_copy(
                part_s.at[2 * b + 1 - core, c], twin_r.at[b, c],
                send_sem.at[7], pair_sem.at[c], twin, MESH,
            ).start()
            return carry

        lax.fori_loop(0, n_y, twin_part, 0)
    sent.append((twin_r, send_sem.at[7]))

    def pair(c):
        wait_recv(twin_r.at[:, c], pair_sem.at[c])

        def body(o, carry):
            there = y_at(o)
            mine = part_s[2 * there + core, c].astype(F32)
            pair_s[there, c] = (mine + twin_r[there, c].astype(F32)).astype(BF)
            pltpu.make_async_remote_copy(
                pair_s.at[there, c], part_r.at[o - 1, c],
                send_sem.at[4], rs_sem.at[c], y_peer(o), MESH,
            ).start()
            return carry

        lax.fori_loop(1, n_y, body, 0)

    for c in range(chunks):
        pair(c)
    for c in range(chunks):
        summed = part_s[j, c].astype(F32) + twin_r[y, c].astype(F32)
        wait_recv(part_r.at[:, c], rs_sem.at[c])
        for o in range(n_y - 1):
            summed = summed + part_r[o, c].astype(F32)
        summed = summed.astype(BF)
        both = jnp.concatenate(
            [
                summed[..., :LANES].reshape(size // 2, LANES),
                summed[..., LANES:].reshape(size // 2, LANES),
            ],
            axis=0,
        )
        tiles = dot(perm[...], both).astype(BF)
        back_s[c * depth : (c + 1) * depth] = tiles.reshape(depth, 16, LANES)
        z_send(c, back_s, back_r, -1, send_sem.at[5], zb_sem)
    sent.append((part_r, send_sem.at[4]))
    sent.append((back_s.at[pl.ds(0, n_h - 1)], send_sem.at[5]))
    back_r[home] = back_s[home]

    wait_recv(xg_r.at[pl.ds(0, n_g - 1), 0], xg_sem)

    def rows_on(o, carry):
        there = lax.rem(g + o, n_g)
        pltpu.make_async_remote_copy(
            xg_r.at[there, core], xg_r.at[there, core],
            send_sem.at[8], xt_sem, twin, MESH,
        ).start()
        return carry

    lax.fori_loop(1, n_g, rows_on, 0)
    sent.append((xg_r.at[pl.ds(0, n_g - 1), 0], send_sem.at[8]))
    xg_r[g] = acts[pl.ds(g * 2, 2)]
    wait_recv(hr.at[pl.ds(0, n_g - 1)], hr_sem)
    wait_recv(xg_r.at[pl.ds(0, n_g - 1), 0], xt_sem)
    for e in range(2):
        mine = slice(e * units, (e + 1) * units)
        ups = [hr[:, n, :, mine].reshape(n_g * m, units) for n in range(3)]
        for b in range(2):
            cols = slice(b * width, (b + 1) * width)
            x = xg_r[:, b, :, 0, e].reshape(n_g * m, width)
            gated = xg_r[:, b, :, 1, e].reshape(n_g * m, width)
            og[e, :, cols] = dot(ups[1], x, TN)
            ou[e, :, cols] = dot(ups[2], x, TN)
            od[e, :, cols] = dot(ups[0], gated, TN)
    stores = [
        pltpu.make_async_copy(src, dst, out_sem.at[n])
        for n, (src, dst) in enumerate(
            (
                (og, gg_hbm),
                (ou, gu_hbm),
                (od, gd_hbm),
                (mixed, mixed_hbm),
                (gtok, gtok_hbm),
            )
        )
    ]
    for store in stores[:3]:
        store.start()

    wait_recv(back_r.at[pl.ds(0, n_h - 1)], zb_sem)
    sums = dot(sel[...], back_r[...].reshape(total, LANES))
    at = [sums[n * toks : (n + 1) * toks] for n in range(8)]
    gtok[:, :LANES] = at[0].astype(BF)
    gtok[:, LANES:] = at[1].astype(BF)
    mixed[:, :LANES] = (at[2] + at[4] + at[6]).astype(BF)
    mixed[:, LANES:] = (at[3] + at[5] + at[7]).astype(BF)

    for store in stores[3:]:
        store.start()

    for ref, sem in sent:
        wait_send(ref, sem)
    for store in stores:
        store.wait()


def hand_over(a, b, c, d, e, ao, bo, co, do, eo, av, bv, cv, dv, ev, get_sem, put_sem):
    gets, puts = [], []
    for n, (src, held, dst) in enumerate(
        ((a, av, ao), (b, bv, bo), (c, cv, co), (d, dv, do), (e, ev, eo))
    ):
        gets.append(pltpu.make_async_copy(src, held, get_sem.at[n]))
        puts.append(pltpu.make_async_copy(held, dst, put_sem.at[n]))
    for get in gets:
        get.start()
    for get, put in zip(gets, puts, strict=True):
        get.wait()
        put.start()
    for put in puts:
        put.wait()


def layer(tokens, grad_mixed, expert_ids, gate_weight, w_gate, w_up, w_down):
    expert_ids, gate_weight = expert_ids.T, gate_weight.T
    w_gate, w_up = jnp.swapaxes(w_gate, 1, 2), jnp.swapaxes(w_up, 1, 2)
    n_g, n_j, n_h = (lax.axis_size(a) for a in ("group", "ingroup", "hid"))
    per, units, d_model = w_gate.shape
    top, toks = expert_ids.shape
    depth = min(8, n_h // 2)
    chunks = n_h // depth
    rows = depth * CAP
    width = 2 * LANES
    m = chunks * rows
    share = d_model // n_g
    hbm = pl.BlockSpec(memory_space=pl.ANY)
    block = (chunks, 2, per, rows, width)
    dma = pltpu.SemaphoreType.DMA
    outs = pl.pallas_call(
        functools.partial(kernel, (n_g, n_j, n_h, chunks, depth, per, top)),
        out_shape=(
            jax.ShapeDtypeStruct((toks, width), BF),
            jax.ShapeDtypeStruct((toks, width), BF),
            jax.ShapeDtypeStruct((per, units, share), F32),
            jax.ShapeDtypeStruct((per, units, share), F32),
            jax.ShapeDtypeStruct((per, units, share), F32),
        ),
        in_specs=[hbm] * 7,
        out_specs=(hbm,) * 5,
        scratch_shapes=[
            pltpu.VMEM((top, toks), jnp.int32),
            pltpu.VMEM((top, toks), F32),
            pltpu.VMEM((toks, width), BF),
            pltpu.VMEM((toks, width), BF),
            pltpu.VMEM(w_gate.shape, BF),
            pltpu.VMEM(w_up.shape, BF),
            pltpu.VMEM(w_down.shape, BF),
            pltpu.VMEM((8 * toks, n_h * 16), BF),
            pltpu.VMEM((depth * 16, depth * 16), BF),
            pltpu.VMEM((depth * 16, depth * 16), BF),
            pltpu.VMEM((n_h, 16, LANES), BF),
            pltpu.VMEM((n_h, 16, LANES), BF),
            pltpu.VMEM((n_j, *block), BF),
            pltpu.VMEM((n_j, *block), BF),
            pltpu.VMEM((n_j // 2, *block), BF),
            pltpu.VMEM((n_j // 2, *block), BF),
            pltpu.VMEM((n_j // 2 - 1, *block), BF),
            pltpu.VMEM((n_h, 16, LANES), BF),
            pltpu.VMEM((n_h, 16, LANES), BF),
            pltpu.VMEM((n_g, 2, *block), BF),
            pltpu.VMEM((n_g, 3, m, per * units), BF),
            pltpu.VMEM((toks, width), BF),
            pltpu.VMEM((toks, width), BF),
            pltpu.VMEM((per, units, share), F32),
            pltpu.VMEM((per, units, share), F32),
            pltpu.VMEM((per, units, share), F32),
            dma((7,)),
            dma((5,)),
            dma((9,)),
            dma((chunks,)),
            dma((chunks,)),
            dma,
            dma((chunks,)),
            dma((chunks,)),
            dma,
            dma,
            dma,
            dma,
        ],
        compiler_params=pltpu.CompilerParams(
            collective_id=0, has_side_effects=True, vmem_limit_bytes=60 * 2**20
        ),
    )(expert_ids, gate_weight, tokens, grad_mixed, w_gate, w_up, w_down)
    mixed, gtok, gg, gu, gd = pl.pallas_call(
        hand_over,
        out_shape=tuple(jax.ShapeDtypeStruct(o.shape, o.dtype) for o in outs),
        in_specs=[hbm] * 5,
        out_specs=(hbm,) * 5,
        scratch_shapes=[*(pltpu.VMEM(o.shape, o.dtype) for o in outs), dma((5,)), dma((5,))],
    )(*outs)
    return mixed, gtok, jnp.swapaxes(gg, 1, 2), jnp.swapaxes(gu, 1, 2), gd


def solution(mesh):
    both = P(("group", "hid"), None)
    return jax.shard_map(
        layer,
        mesh=mesh,
        in_specs=(
            both,
            both,
            both,
            both,
            P("hid", None, "ingroup"),
            P("hid", None, "ingroup"),
            P("hid", "ingroup", None),
        ),
        out_specs=(
            P(("group", "hid"), "ingroup"),
            P(("group", "hid"), "ingroup"),
            P("hid", "group", "ingroup"),
            P("hid", "group", "ingroup"),
            P("hid", "ingroup", "group"),
        ),
        check_vma=False,
    )
```

```python
import functools

import jax
import jax.numpy as jnp
from jax import lax
from jax.experimental import pallas as pl
from jax.experimental.pallas import tpu as pltpu
from jax.sharding import PartitionSpec as P

MESH = pl.DeviceIdType.MESH
BF = jnp.bfloat16
F32 = jnp.float32
CAP = 2
LANES = 128

NN = (((1,), (0,)), ((), ()))
NT = (((1,), (1,)), ((), ()))
TN = (((0,), (0,)), ((), ()))


def dot(a, b, dims=NN):
    return lax.dot_general(a, b, dims, preferred_element_type=F32)


def iota(shape, dim):
    return lax.broadcasted_iota(jnp.int32, shape, dim)


def kernel(
    dims,
    ids_hbm, gw_hbm, tok_hbm, grd_hbm, wg_hbm, wu_hbm, wd_hbm,
    mixed_hbm, gtok_hbm, gg_hbm, gu_hbm, gd_hbm,
    ids, gw, tok, grd, wg, wu, wd, sel, unperm, perm,
    tile_s, tile_r, relay, acts, part_s, twin_r, pair_s, part_r, back_s, back_r,
    xg_r, hr, mixed, gtok, og, ou, od,
    in_sem, out_sem, send_sem, relay_sem, z_sem, y_sem, twin_sem, pair_sem, rs_sem, zb_sem, xg_sem, xt_sem, hr_sem,
):
    n_g, n_j, n_h, chunks, depth, per, top = dims
    rows = depth * CAP
    half = depth // 2
    toks = ids_hbm.shape[1]
    g, j, h = lax.axis_index("group"), lax.axis_index("ingroup"), lax.axis_index("hid")
    width = 2 * LANES

    lanes = pl.ds(pl.multiple_of(j * width, width), width)
    loads = [
        pltpu.make_async_copy(src, dst, in_sem.at[n])
        for n, (src, dst) in enumerate(
            (
                (ids_hbm, ids),
                (gw_hbm, gw),
                (tok_hbm.at[:, lanes], tok),
                (grd_hbm.at[:, lanes], grd),
                (wg_hbm, wg),
                (wu_hbm, wu),
                (wd_hbm, wd),
            )
        )
    ]
    for load in loads:
        load.start()
    sent = []

    barrier = pltpu.get_barrier_semaphore()

    def greet(count, device):
        def body(o, carry):
            pl.semaphore_signal(
                barrier, inc=1, device_id=device(o), device_id_type=MESH
            )
            return carry

        lax.fori_loop(1, count, body, 0)

    def hid_peer(o):
        return (g, j, lax.rem(h + o, n_h))

    n_y, y, core = n_j // 2, j // 2, j % 2
    twin = (g, 2 * y + 1 - core, h)

    def y_at(o):
        return lax.rem(y + o, n_y)

    def y_peer(o):
        return (g, 2 * y_at(o) + core, h)

    def group_peer(o):
        return (lax.rem(g + o, n_g), j, h)

    greet(n_h // 4 + 1, hid_peer)
    greet(n_h // 4 + 1, lambda o: hid_peer(n_h - o))
    greet(n_y, y_peer)
    pl.semaphore_signal(barrier, inc=1, device_id=twin, device_id_type=MESH)
    greet(n_g, group_peer)

    total = n_h * 16
    lane = iota((1, total), 1)
    pos = lane // 16
    which, part = (lane // 8) % 2, (lane // 4) % 2
    expert_local, place = (lane // 2) % 2, lane % 2
    ck, i = pos // depth, pos % depth
    delta = jnp.where(
        i < half, n_h // 2 - half * (ck + 1) + i, n_h // 2 + half * ck + i - half
    )
    expert = ((h + delta) % n_h) * 2 + expert_local
    named = jnp.zeros((toks, total), F32)
    gates = jnp.zeros((toks, total), F32)
    loads[0].wait()
    loads[1].wait()
    same = iota((toks, toks), 0) == iota((toks, toks), 1)

    def column(row):
        return jnp.sum(jnp.where(same, row.astype(F32), 0.0), axis=1, keepdims=True)

    wanted = expert.astype(F32)
    for k in range(top):
        hit = (column(ids[k : k + 1, :]) == wanted).astype(F32)
        named = named + hit
        gates = gates + hit * column(gw[k : k + 1, :])
    earlier = (iota((toks, toks), 1) < iota((toks, toks), 0)).astype(BF)
    rank = dot(earlier, named.astype(BF))
    taken = named * (rank == place.astype(F32)).astype(F32)
    gates = gates * taken
    hi = gates.astype(BF)
    rest = gates - hi.astype(F32)
    mid = rest.astype(BF)
    lo = (rest - mid.astype(F32)).astype(BF)
    pick = taken.astype(BF)
    pieces = []
    for value, w in ((pick, 0), (hi, 1), (mid, 1), (lo, 1)):
        for p in range(2):
            pieces.append(value * ((which == w) & (part == p)).astype(BF))
    sel[...] = jnp.concatenate(pieces, axis=0)

    size = depth * 16

    def row_order(q):
        p, w = q // (size // 2), (q // (size // 4)) % 2
        e, t, c = (q // rows) % 2, (q // CAP) % depth, q % CAP
        return t * 16 + w * 8 + p * 4 + e * 2 + c

    unperm[...] = (row_order(iota((size, size), 0)) == iota((size, size), 1)).astype(BF)
    perm[...] = (row_order(iota((size, size), 1)) == iota((size, size), 0)).astype(BF)

    loads[2].wait()
    loads[3].wait()
    t0, t1 = tok[:, :LANES], tok[:, LANES:]
    g0, g1 = grd[:, :LANES], grd[:, LANES:]
    rhs = jnp.concatenate([t0, t1, g0, g1, g0, g1, g0, g1], axis=0)
    tile_s[...] = dot(sel[...], rhs, TN).astype(BF).reshape(n_h, 16, LANES)
    home = (chunks - 1) * depth
    tile_r[home] = tile_s[home]

    pl.semaphore_wait(barrier, n_h // 4 * 2 + n_y - 1 + 1 + n_g - 1)

    def wait_recv(ref, sem):
        pltpu.make_async_remote_copy(ref, ref, sem, sem, twin, MESH).wait_recv()

    def wait_send(ref, sem):
        pltpu.make_async_remote_copy(ref, ref, sem, sem, twin, MESH).wait_send()

    def distance(c, t):
        return jnp.where(
            t < half, n_h // 2 - half * (c + 1) + t, n_h // 2 + half * c + t - half
        )

    def z_send(c, src, dst, sign, send, recv):
        def body(t, carry):
            t = jnp.where(t % 2 == 0, t // 2, depth - 1 - t // 2)
            at = c * depth + t
            peer = lax.rem(h + n_h + sign * distance(c, t), n_h)
            pltpu.make_async_remote_copy(
                src.at[at], dst.at[at], send, recv, (g, j, peer), MESH
            ).start()
            return carry

        lax.fori_loop(1 if c == chunks - 1 else 0, depth, body, 0)

    def z_block(c, ref):
        own = c in (chunks // 2 - 1, chunks - 1)
        return ref.at[pl.ds(c * depth + own, depth - own)]

    reach, last = n_h // 4, chunks - 1
    outer = chunks // 2

    def side(c, up):
        return pl.ds(c * depth + (0 if up else half), half)

    def via(up):
        return (g, j, lax.rem(h + (reach if up else n_h - reach), n_h))

    for c in range(outer):
        for up in (True, False):
            pltpu.make_async_remote_copy(
                tile_s.at[side(c, up)], relay.at[side(c, up)],
                send_sem.at[0], relay_sem.at[2 * c + (not up)], via(up), MESH,
            ).start()
    for c in range(last, outer - 1, -1):
        z_send(c, tile_s, tile_r, 1, send_sem.at[0], z_sem.at[c])
    sent.append((tile_s.at[pl.ds(0, n_h - 1)], send_sem.at[0]))
    for c in range(outer):
        for up in (True, False):
            wait_recv(relay.at[side(c, up)], relay_sem.at[2 * c + (not up)])

            def onward(t, carry, c=c, up=up):
                at = c * depth + t + (0 if up else half)
                away = half * (outer - 1 - c) + t if up else n_h - reach + half * c + t
                pltpu.make_async_remote_copy(
                    relay.at[at], tile_r.at[at], send_sem.at[9], z_sem.at[c],
                    (g, j, lax.rem(h + away, n_h)), MESH,
                ).start()
                return carry

            mine = up and c == outer - 1
            lax.fori_loop(1 if mine else 0, half, onward, 0)
            if mine:
                tile_r[c * depth] = relay[c * depth]
    sent.append((relay.at[pl.ds(0, n_h // 2 - 1)], send_sem.at[9]))

    def to_twin(b, c):
        pltpu.make_async_remote_copy(
            acts.at[b, c], acts.at[b, c], send_sem.at[6], twin_sem, twin, MESH
        ).start()

    def pass_on(c):
        wait_recv(acts.at[pl.ds(0, n_y - 1), c], y_sem.at[c])

        def body(o, carry):
            to_twin(2 * y_at(o) + core, c)
            return carry

        lax.fori_loop(1, n_y, body, 0)

    order = [*range(last, outer - 1, -1), *range(outer)]
    for c in order:
        wait_recv(z_block(c, tile_r), z_sem.at[c])
        tiles = tile_r[c * depth : (c + 1) * depth].reshape(size, LANES)
        ordered = dot(unperm[...], tiles).astype(BF)
        acts[j, c, :, :, :, :LANES] = ordered[: size // 2].reshape(2, 2, rows, LANES)
        acts[j, c, :, :, :, LANES:] = ordered[size // 2 :].reshape(2, 2, rows, LANES)

        def forward(o, carry, c=c):
            pltpu.make_async_remote_copy(
                acts.at[j, c], acts.at[j, c],
                send_sem.at[1], y_sem.at[c], y_peer(o), MESH,
            ).start()
            return carry

        lax.fori_loop(1, n_y, forward, 0)
        to_twin(j, c)
    for c in order:
        pass_on(c)
    sent.append((acts.at[pl.ds(0, n_y - 1)], send_sem.at[1]))
    sent.append((acts.at[pl.ds(0, n_y)], send_sem.at[6]))
    for load in loads[4:]:
        load.wait()
    wait_recv(acts.at[pl.ds(0, n_y)], twin_sem)


    def rows_out(o, carry):
        there = lax.rem(g + o, n_g)
        pltpu.make_async_remote_copy(
            acts.at[2 * there + core], xg_r.at[g, core],
            send_sem.at[2], xg_sem, (there, j, h), MESH,
        ).start()
        return carry

    lax.fori_loop(1, n_g, rows_out, 0)
    sent.append((xg_r.at[pl.ds(0, n_g - 1), 0], send_sem.at[2]))

    m = chunks * rows
    units = wg.shape[1]
    hiddens = []
    for e in range(2):
        gate_pre = jnp.zeros((m, units), F32)
        up_pre = jnp.zeros((m, units), F32)
        d_hidden = jnp.zeros((m, units), F32)
        for b in range(n_j):
            cols = slice(b * width, (b + 1) * width)
            x = acts[b, :, 0, e].reshape(m, width)
            gated = acts[b, :, 1, e].reshape(m, width)
            gate_pre = gate_pre + dot(x, wg[e, :, cols], NT)
            up_pre = up_pre + dot(x, wu[e, :, cols], NT)
            d_hidden = d_hidden + dot(gated, wd[e, :, cols], NT)
        sig = jax.nn.sigmoid(gate_pre)
        silu = gate_pre * sig
        d_gate = d_hidden * up_pre * sig * (1.0 + gate_pre * (1.0 - sig))
        hiddens.append(
            [v.astype(BF) for v in (silu * up_pre, d_gate, d_hidden * silu)]
        )
    for n in range(3):
        hr[g, n] = jnp.concatenate([hiddens[0][n], hiddens[1][n]], axis=1)

    def hidden_out(o, carry):
        pltpu.make_async_remote_copy(
            hr.at[g], hr.at[g], send_sem.at[3], hr_sem, group_peer(o), MESH
        ).start()
        return carry

    lax.fori_loop(1, n_g, hidden_out, 0)
    sent.append((hr.at[pl.ds(0, n_g - 1)], send_sem.at[3]))

    for e in range(2):
        hidden, d_gate, d_up = hiddens[e]
        for b in range(n_j):
            cols = slice(b * width, (b + 1) * width)
            out = dot(hidden, wd[e, :, cols]).astype(BF)
            part_s[b, :, 1, e] = out.reshape(chunks, rows, width)
            back = dot(d_gate, wg[e, :, cols]) + dot(d_up, wu[e, :, cols])
            part_s[b, :, 0, e] = back.astype(BF).reshape(chunks, rows, width)

    for c in range(chunks):

        def twin_part(b, carry, c=c):
            pltpu.make_async_remote_copy(
                part_s.at[2 * b + 1 - core, c], twin_r.at[b, c],
                send_sem.at[7], pair_sem.at[c], twin, MESH,
            ).start()
            return carry

        lax.fori_loop(0, n_y, twin_part, 0)
    sent.append((twin_r, send_sem.at[7]))

    def pair(c):
        wait_recv(twin_r.at[:, c], pair_sem.at[c])

        def body(o, carry):
            there = y_at(o)
            mine = part_s[2 * there + core, c].astype(F32)
            pair_s[there, c] = (mine + twin_r[there, c].astype(F32)).astype(BF)
            pltpu.make_async_remote_copy(
                pair_s.at[there, c], part_r.at[o - 1, c],
                send_sem.at[4], rs_sem.at[c], y_peer(o), MESH,
            ).start()
            return carry

        lax.fori_loop(1, n_y, body, 0)

    for c in range(chunks):
        pair(c)
    for c in range(chunks):
        summed = part_s[j, c].astype(F32) + twin_r[y, c].astype(F32)
        wait_recv(part_r.at[:, c], rs_sem.at[c])
        for o in range(n_y - 1):
            summed = summed + part_r[o, c].astype(F32)
        summed = summed.astype(BF)
        both = jnp.concatenate(
            [
                summed[..., :LANES].reshape(size // 2, LANES),
                summed[..., LANES:].reshape(size // 2, LANES),
            ],
            axis=0,
        )
        tiles = dot(perm[...], both).astype(BF)
        back_s[c * depth : (c + 1) * depth] = tiles.reshape(depth, 16, LANES)
        z_send(c, back_s, back_r, -1, send_sem.at[5], zb_sem)
    sent.append((part_r, send_sem.at[4]))
    sent.append((back_s.at[pl.ds(0, n_h - 1)], send_sem.at[5]))
    back_r[home] = back_s[home]

    wait_recv(xg_r.at[pl.ds(0, n_g - 1), 0], xg_sem)

    def rows_on(o, carry):
        there = lax.rem(g + o, n_g)
        pltpu.make_async_remote_copy(
            xg_r.at[there, core], xg_r.at[there, core],
            send_sem.at[8], xt_sem, twin, MESH,
        ).start()
        return carry

    lax.fori_loop(1, n_g, rows_on, 0)
    sent.append((xg_r.at[pl.ds(0, n_g - 1), 0], send_sem.at[8]))
    xg_r[g] = acts[pl.ds(g * 2, 2)]
    wait_recv(hr.at[pl.ds(0, n_g - 1)], hr_sem)
    wait_recv(xg_r.at[pl.ds(0, n_g - 1), 0], xt_sem)
    for e in range(2):
        mine = slice(e * units, (e + 1) * units)
        ups = [hr[:, n, :, mine].reshape(n_g * m, units) for n in range(3)]
        for b in range(2):
            cols = slice(b * width, (b + 1) * width)
            x = xg_r[:, b, :, 0, e].reshape(n_g * m, width)
            gated = xg_r[:, b, :, 1, e].reshape(n_g * m, width)
            og[e, :, cols] = dot(ups[1], x, TN)
            ou[e, :, cols] = dot(ups[2], x, TN)
            od[e, :, cols] = dot(ups[0], gated, TN)
    stores = [
        pltpu.make_async_copy(src, dst, out_sem.at[n])
        for n, (src, dst) in enumerate(
            (
                (og, gg_hbm),
                (ou, gu_hbm),
                (od, gd_hbm),
                (mixed, mixed_hbm),
                (gtok, gtok_hbm),
            )
        )
    ]
    for store in stores[:3]:
        store.start()

    wait_recv(back_r.at[pl.ds(0, n_h - 1)], zb_sem)
    sums = dot(sel[...], back_r[...].reshape(total, LANES))
    at = [sums[n * toks : (n + 1) * toks] for n in range(8)]
    gtok[:, :LANES] = at[0].astype(BF)
    gtok[:, LANES:] = at[1].astype(BF)
    mixed[:, :LANES] = (at[2] + at[4] + at[6]).astype(BF)
    mixed[:, LANES:] = (at[3] + at[5] + at[7]).astype(BF)

    for store in stores[3:]:
        store.start()

    for ref, sem in sent:
        wait_send(ref, sem)
    for store in stores:
        store.wait()


def hand_over(a, b, c, d, e, ao, bo, co, do, eo, av, bv, cv, dv, ev, get_sem, put_sem):
    gets, puts = [], []
    for n, (src, held, dst) in enumerate(
        ((a, av, ao), (b, bv, bo), (c, cv, co), (d, dv, do), (e, ev, eo))
    ):
        gets.append(pltpu.make_async_copy(src, held, get_sem.at[n]))
        puts.append(pltpu.make_async_copy(held, dst, put_sem.at[n]))
    for get in gets:
        get.start()
    for get, put in zip(gets, puts, strict=True):
        get.wait()
        put.start()
    for put in puts:
        put.wait()


def layer(tokens, grad_mixed, expert_ids, gate_weight, w_gate, w_up, w_down):
    expert_ids, gate_weight = expert_ids.T, gate_weight.T
    w_gate, w_up = jnp.swapaxes(w_gate, 1, 2), jnp.swapaxes(w_up, 1, 2)
    n_g, n_j, n_h = (lax.axis_size(a) for a in ("group", "ingroup", "hid"))
    per, units, d_model = w_gate.shape
    top, toks = expert_ids.shape
    depth = min(8, n_h // 2)
    chunks = n_h // depth
    rows = depth * CAP
    width = 2 * LANES
    m = chunks * rows
    share = d_model // n_g
    hbm = pl.BlockSpec(memory_space=pl.ANY)
    block = (chunks, 2, per, rows, width)
    dma = pltpu.SemaphoreType.DMA
    outs = pl.pallas_call(
        functools.partial(kernel, (n_g, n_j, n_h, chunks, depth, per, top)),
        out_shape=(
            jax.ShapeDtypeStruct((toks, width), BF),
            jax.ShapeDtypeStruct((toks, width), BF),
            jax.ShapeDtypeStruct((per, units, share), F32),
            jax.ShapeDtypeStruct((per, units, share), F32),
            jax.ShapeDtypeStruct((per, units, share), F32),
        ),
        in_specs=[hbm] * 7,
        out_specs=(hbm,) * 5,
        scratch_shapes=[
            pltpu.VMEM((top, toks), jnp.int32),
            pltpu.VMEM((top, toks), F32),
            pltpu.VMEM((toks, width), BF),
            pltpu.VMEM((toks, width), BF),
            pltpu.VMEM(w_gate.shape, BF),
            pltpu.VMEM(w_up.shape, BF),
            pltpu.VMEM(w_down.shape, BF),
            pltpu.VMEM((8 * toks, n_h * 16), BF),
            pltpu.VMEM((depth * 16, depth * 16), BF),
            pltpu.VMEM((depth * 16, depth * 16), BF),
            pltpu.VMEM((n_h, 16, LANES), BF),
            pltpu.VMEM((n_h, 16, LANES), BF),
            pltpu.VMEM((n_h // 2, 16, LANES), BF),
            pltpu.VMEM((n_j, *block), BF),
            pltpu.VMEM((n_j, *block), BF),
            pltpu.VMEM((n_j // 2, *block), BF),
            pltpu.VMEM((n_j // 2, *block), BF),
            pltpu.VMEM((n_j // 2 - 1, *block), BF),
            pltpu.VMEM((n_h, 16, LANES), BF),
            pltpu.VMEM((n_h, 16, LANES), BF),
            pltpu.VMEM((n_g, 2, *block), BF),
            pltpu.VMEM((n_g, 3, m, per * units), BF),
            pltpu.VMEM((toks, width), BF),
            pltpu.VMEM((toks, width), BF),
            pltpu.VMEM((per, units, share), F32),
            pltpu.VMEM((per, units, share), F32),
            pltpu.VMEM((per, units, share), F32),
            dma((7,)),
            dma((5,)),
            dma((10,)),
            dma((chunks,)),
            dma((chunks,)),
            dma((chunks,)),
            dma,
            dma((chunks,)),
            dma((chunks,)),
            dma,
            dma,
            dma,
            dma,
        ],
        compiler_params=pltpu.CompilerParams(
            collective_id=0, has_side_effects=True, vmem_limit_bytes=60 * 2**20
        ),
    )(expert_ids, gate_weight, tokens, grad_mixed, w_gate, w_up, w_down)
    mixed, gtok, gg, gu, gd = pl.pallas_call(
        hand_over,
        out_shape=tuple(jax.ShapeDtypeStruct(o.shape, o.dtype) for o in outs),
        in_specs=[hbm] * 5,
        out_specs=(hbm,) * 5,
        scratch_shapes=[*(pltpu.VMEM(o.shape, o.dtype) for o in outs), dma((5,)), dma((5,))],
    )(*outs)
    return mixed, gtok, jnp.swapaxes(gg, 1, 2), jnp.swapaxes(gu, 1, 2), gd


def solution(mesh):
    both = P(("group", "hid"), None)
    return jax.shard_map(
        layer,
        mesh=mesh,
        in_specs=(
            both,
            both,
            both,
            both,
            P("hid", None, "ingroup"),
            P("hid", None, "ingroup"),
            P("hid", "ingroup", None),
        ),
        out_specs=(
            P(("group", "hid"), "ingroup"),
            P(("group", "hid"), "ingroup"),
            P("hid", "group", "ingroup"),
            P("hid", "group", "ingroup"),
            P("hid", "ingroup", "group"),
        ),
        check_vma=False,
    )
```

```python
import functools

import jax
import jax.numpy as jnp
from jax import lax
from jax.experimental import pallas as pl
from jax.experimental.pallas import tpu as pltpu
from jax.sharding import PartitionSpec as P

MESH = pl.DeviceIdType.MESH
BF = jnp.bfloat16
F32 = jnp.float32
CAP = 2
LANES = 128

NN = (((1,), (0,)), ((), ()))
NT = (((1,), (1,)), ((), ()))
TN = (((0,), (0,)), ((), ()))


def dot(a, b, dims=NN):
    return lax.dot_general(a, b, dims, preferred_element_type=F32)


def iota(shape, dim):
    return lax.broadcasted_iota(jnp.int32, shape, dim)


def kernel(
    dims,
    ids_hbm, gw_hbm, tok_hbm, grd_hbm, wg_hbm, wu_hbm, wd_hbm,
    mixed_hbm, gtok_hbm, gg_hbm, gu_hbm, gd_hbm,
    ids, gw, tok, grd, wg, wu, wd, sel, unperm, perm,
    tile_s, tile_r, relay, acts, part_s, twin_r, pair_s, part_r, back_s, back_r,
    xg_r, hr, mixed, gtok, og, ou, od,
    in_sem, out_sem, send_sem, relay_sem, z_sem, y_sem, twin_sem, pair_sem, rs_sem, zb_sem, xg_sem, xt_sem, hr_sem,
):
    n_g, n_j, n_h, chunks, depth, per, top = dims
    rows = depth * CAP
    half = depth // 2
    toks = ids_hbm.shape[1]
    g, j, h = lax.axis_index("group"), lax.axis_index("ingroup"), lax.axis_index("hid")
    width = 2 * LANES

    lanes = pl.ds(pl.multiple_of(j * width, width), width)
    loads = [
        pltpu.make_async_copy(src, dst, in_sem.at[n])
        for n, (src, dst) in enumerate(
            (
                (ids_hbm, ids),
                (gw_hbm, gw),
                (tok_hbm.at[:, lanes], tok),
                (grd_hbm.at[:, lanes], grd),
                (wg_hbm, wg),
                (wu_hbm, wu),
                (wd_hbm, wd),
            )
        )
    ]
    for load in loads:
        load.start()
    sent = []

    barrier = pltpu.get_barrier_semaphore()

    def greet(count, device):
        def body(o, carry):
            pl.semaphore_signal(
                barrier, inc=1, device_id=device(o), device_id_type=MESH
            )
            return carry

        lax.fori_loop(1, count, body, 0)

    def hid_peer(o):
        return (g, j, lax.rem(h + o, n_h))

    n_y, y, core = n_j // 2, j // 2, j % 2
    twin = (g, 2 * y + 1 - core, h)

    def y_at(o):
        return lax.rem(y + o, n_y)

    def y_peer(o):
        return (g, 2 * y_at(o) + core, h)

    def group_peer(o):
        return (lax.rem(g + o, n_g), j, h)

    greet(n_h // 4 + 1, hid_peer)
    greet(n_h // 4 + 1, lambda o: hid_peer(n_h - o))
    greet(n_y, y_peer)
    pl.semaphore_signal(barrier, inc=1, device_id=twin, device_id_type=MESH)
    greet(n_g, group_peer)

    total = n_h * 16
    lane = iota((1, total), 1)
    pos = lane // 16
    which, part = (lane // 8) % 2, (lane // 4) % 2
    expert_local, place = (lane // 2) % 2, lane % 2
    ck, i = pos // depth, pos % depth
    delta = jnp.where(
        i < half, n_h // 2 - half * (ck + 1) + i, n_h // 2 + half * ck + i - half
    )
    expert = ((h + delta) % n_h) * 2 + expert_local
    named = jnp.zeros((toks, total), F32)
    gates = jnp.zeros((toks, total), F32)
    loads[0].wait()
    loads[1].wait()
    same = iota((toks, toks), 0) == iota((toks, toks), 1)

    def column(row):
        return jnp.sum(jnp.where(same, row.astype(F32), 0.0), axis=1, keepdims=True)

    wanted = expert.astype(F32)
    for k in range(top):
        hit = (column(ids[k : k + 1, :]) == wanted).astype(F32)
        named = named + hit
        gates = gates + hit * column(gw[k : k + 1, :])
    earlier = (iota((toks, toks), 1) < iota((toks, toks), 0)).astype(BF)
    rank = dot(earlier, named.astype(BF))
    taken = named * (rank == place.astype(F32)).astype(F32)
    gates = gates * taken
    hi = gates.astype(BF)
    rest = gates - hi.astype(F32)
    mid = rest.astype(BF)
    lo = (rest - mid.astype(F32)).astype(BF)
    pick = taken.astype(BF)
    pieces = []
    for value, w in ((pick, 0), (hi, 1), (mid, 1), (lo, 1)):
        for p in range(2):
            pieces.append(value * ((which == w) & (part == p)).astype(BF))
    sel[...] = jnp.concatenate(pieces, axis=0)

    size = depth * 16

    def row_order(q):
        p, w = q // (size // 2), (q // (size // 4)) % 2
        e, t, c = (q // rows) % 2, (q // CAP) % depth, q % CAP
        return t * 16 + w * 8 + p * 4 + e * 2 + c

    unperm[...] = (row_order(iota((size, size), 0)) == iota((size, size), 1)).astype(BF)
    perm[...] = (row_order(iota((size, size), 1)) == iota((size, size), 0)).astype(BF)

    loads[2].wait()
    loads[3].wait()
    t0, t1 = tok[:, :LANES], tok[:, LANES:]
    g0, g1 = grd[:, :LANES], grd[:, LANES:]
    rhs = jnp.concatenate([t0, t1, g0, g1, g0, g1, g0, g1], axis=0)
    tile_s[...] = dot(sel[...], rhs, TN).astype(BF).reshape(n_h, 16, LANES)
    home = (chunks - 1) * depth
    tile_r[home] = tile_s[home]

    pl.semaphore_wait(barrier, n_h // 4 * 2 + n_y - 1 + 1 + n_g - 1)

    def wait_recv(ref, sem):
        pltpu.make_async_remote_copy(ref, ref, sem, sem, twin, MESH).wait_recv()

    def wait_send(ref, sem):
        pltpu.make_async_remote_copy(ref, ref, sem, sem, twin, MESH).wait_send()

    def distance(c, t):
        return jnp.where(
            t < half, n_h // 2 - half * (c + 1) + t, n_h // 2 + half * c + t - half
        )

    def z_send(c, src, dst, sign, send, recv):
        def body(t, carry):
            t = jnp.where(t % 2 == 0, t // 2, depth - 1 - t // 2)
            at = c * depth + t
            peer = lax.rem(h + n_h + sign * distance(c, t), n_h)
            pltpu.make_async_remote_copy(
                src.at[at], dst.at[at], send, recv, (g, j, peer), MESH
            ).start()
            return carry

        lax.fori_loop(1 if c == chunks - 1 else 0, depth, body, 0)

    def z_block(c, ref):
        own = c in (chunks // 2 - 1, chunks - 1)
        return ref.at[pl.ds(c * depth + own, depth - own)]

    reach, last = n_h // 4, chunks - 1
    outer = chunks // 2

    def side(c, up):
        return pl.ds(c * depth + (0 if up else half), half)

    def via(up):
        return (g, j, lax.rem(h + (reach if up else n_h - reach), n_h))

    for c in range(outer):
        for up in (True, False):
            pltpu.make_async_remote_copy(
                tile_s.at[side(c, up)], relay.at[side(c, up)],
                send_sem.at[0], relay_sem.at[2 * c + (not up)], via(up), MESH,
            ).start()
    for c in range(last, outer - 1, -1):
        z_send(c, tile_s, tile_r, 1, send_sem.at[0], z_sem.at[c])
    sent.append((tile_s.at[pl.ds(0, n_h - 1)], send_sem.at[0]))
    def to_twin(b, c):
        pltpu.make_async_remote_copy(
            acts.at[b, c], acts.at[b, c], send_sem.at[6], twin_sem, twin, MESH
        ).start()

    def pass_on(c):
        wait_recv(acts.at[pl.ds(0, n_y - 1), c], y_sem.at[c])

        def body(o, carry):
            to_twin(2 * y_at(o) + core, c)
            return carry

        lax.fori_loop(1, n_y, body, 0)

    order = [*range(last, outer - 1, -1), *range(outer)]
    def take(c):
        wait_recv(z_block(c, tile_r), z_sem.at[c])
        tiles = tile_r[c * depth : (c + 1) * depth].reshape(size, LANES)
        ordered = dot(unperm[...], tiles).astype(BF)
        acts[j, c, :, :, :, :LANES] = ordered[: size // 2].reshape(2, 2, rows, LANES)
        acts[j, c, :, :, :, LANES:] = ordered[size // 2 :].reshape(2, 2, rows, LANES)

        def forward(o, carry, c=c):
            pltpu.make_async_remote_copy(
                acts.at[j, c], acts.at[j, c],
                send_sem.at[1], y_sem.at[c], y_peer(o), MESH,
            ).start()
            return carry

        lax.fori_loop(1, n_y, forward, 0)
        to_twin(j, c)

    take(last)
    for c in range(outer):
        for up in (True, False):
            wait_recv(relay.at[side(c, up)], relay_sem.at[2 * c + (not up)])

            def onward(t, carry, c=c, up=up):
                at = c * depth + t + (0 if up else half)
                away = half * (outer - 1 - c) + t if up else n_h - reach + half * c + t
                pltpu.make_async_remote_copy(
                    relay.at[at], tile_r.at[at], send_sem.at[9], z_sem.at[c],
                    (g, j, lax.rem(h + away, n_h)), MESH,
                ).start()
                return carry

            mine = up and c == outer - 1
            lax.fori_loop(1 if mine else 0, half, onward, 0)
            if mine:
                tile_r[c * depth] = relay[c * depth]
    sent.append((relay.at[pl.ds(0, n_h // 2 - 1)], send_sem.at[9]))
    for c in order[1:]:
        take(c)
    for c in order:
        pass_on(c)
    sent.append((acts.at[pl.ds(0, n_y - 1)], send_sem.at[1]))
    sent.append((acts.at[pl.ds(0, n_y)], send_sem.at[6]))
    for load in loads[4:]:
        load.wait()
    wait_recv(acts.at[pl.ds(0, n_y)], twin_sem)


    def rows_out(o, carry):
        there = lax.rem(g + o, n_g)
        pltpu.make_async_remote_copy(
            acts.at[2 * there + core], xg_r.at[g, core],
            send_sem.at[2], xg_sem, (there, j, h), MESH,
        ).start()
        return carry

    lax.fori_loop(1, n_g, rows_out, 0)
    sent.append((xg_r.at[pl.ds(0, n_g - 1), 0], send_sem.at[2]))

    m = chunks * rows
    units = wg.shape[1]
    hiddens = []
    for e in range(2):
        gate_pre = jnp.zeros((m, units), F32)
        up_pre = jnp.zeros((m, units), F32)
        d_hidden = jnp.zeros((m, units), F32)
        for b in range(n_j):
            cols = slice(b * width, (b + 1) * width)
            x = acts[b, :, 0, e].reshape(m, width)
            gated = acts[b, :, 1, e].reshape(m, width)
            gate_pre = gate_pre + dot(x, wg[e, :, cols], NT)
            up_pre = up_pre + dot(x, wu[e, :, cols], NT)
            d_hidden = d_hidden + dot(gated, wd[e, :, cols], NT)
        sig = jax.nn.sigmoid(gate_pre)
        silu = gate_pre * sig
        d_gate = d_hidden * up_pre * sig * (1.0 + gate_pre * (1.0 - sig))
        hiddens.append(
            [v.astype(BF) for v in (silu * up_pre, d_gate, d_hidden * silu)]
        )
    for n in range(3):
        hr[g, n] = jnp.concatenate([hiddens[0][n], hiddens[1][n]], axis=1)

    def hidden_out(o, carry):
        pltpu.make_async_remote_copy(
            hr.at[g], hr.at[g], send_sem.at[3], hr_sem, group_peer(o), MESH
        ).start()
        return carry

    lax.fori_loop(1, n_g, hidden_out, 0)
    sent.append((hr.at[pl.ds(0, n_g - 1)], send_sem.at[3]))

    for e in range(2):
        hidden, d_gate, d_up = hiddens[e]
        for b in range(n_j):
            cols = slice(b * width, (b + 1) * width)
            out = dot(hidden, wd[e, :, cols]).astype(BF)
            part_s[b, :, 1, e] = out.reshape(chunks, rows, width)
            back = dot(d_gate, wg[e, :, cols]) + dot(d_up, wu[e, :, cols])
            part_s[b, :, 0, e] = back.astype(BF).reshape(chunks, rows, width)

    for c in range(chunks):

        def twin_part(b, carry, c=c):
            pltpu.make_async_remote_copy(
                part_s.at[2 * b + 1 - core, c], twin_r.at[b, c],
                send_sem.at[7], pair_sem.at[c], twin, MESH,
            ).start()
            return carry

        lax.fori_loop(0, n_y, twin_part, 0)
    sent.append((twin_r, send_sem.at[7]))

    def pair(c):
        wait_recv(twin_r.at[:, c], pair_sem.at[c])

        def body(o, carry):
            there = y_at(o)
            mine = part_s[2 * there + core, c].astype(F32)
            pair_s[there, c] = (mine + twin_r[there, c].astype(F32)).astype(BF)
            pltpu.make_async_remote_copy(
                pair_s.at[there, c], part_r.at[o - 1, c],
                send_sem.at[4], rs_sem.at[c], y_peer(o), MESH,
            ).start()
            return carry

        lax.fori_loop(1, n_y, body, 0)

    for c in range(chunks):
        pair(c)
    for c in range(chunks):
        summed = part_s[j, c].astype(F32) + twin_r[y, c].astype(F32)
        wait_recv(part_r.at[:, c], rs_sem.at[c])
        for o in range(n_y - 1):
            summed = summed + part_r[o, c].astype(F32)
        summed = summed.astype(BF)
        both = jnp.concatenate(
            [
                summed[..., :LANES].reshape(size // 2, LANES),
                summed[..., LANES:].reshape(size // 2, LANES),
            ],
            axis=0,
        )
        tiles = dot(perm[...], both).astype(BF)
        back_s[c * depth : (c + 1) * depth] = tiles.reshape(depth, 16, LANES)
        z_send(c, back_s, back_r, -1, send_sem.at[5], zb_sem)
    sent.append((part_r, send_sem.at[4]))
    sent.append((back_s.at[pl.ds(0, n_h - 1)], send_sem.at[5]))
    back_r[home] = back_s[home]

    wait_recv(xg_r.at[pl.ds(0, n_g - 1), 0], xg_sem)

    def rows_on(o, carry):
        there = lax.rem(g + o, n_g)
        pltpu.make_async_remote_copy(
            xg_r.at[there, core], xg_r.at[there, core],
            send_sem.at[8], xt_sem, twin, MESH,
        ).start()
        return carry

    lax.fori_loop(1, n_g, rows_on, 0)
    sent.append((xg_r.at[pl.ds(0, n_g - 1), 0], send_sem.at[8]))
    xg_r[g] = acts[pl.ds(g * 2, 2)]
    wait_recv(hr.at[pl.ds(0, n_g - 1)], hr_sem)
    wait_recv(xg_r.at[pl.ds(0, n_g - 1), 0], xt_sem)
    for e in range(2):
        mine = slice(e * units, (e + 1) * units)
        ups = [hr[:, n, :, mine].reshape(n_g * m, units) for n in range(3)]
        for b in range(2):
            cols = slice(b * width, (b + 1) * width)
            x = xg_r[:, b, :, 0, e].reshape(n_g * m, width)
            gated = xg_r[:, b, :, 1, e].reshape(n_g * m, width)
            og[e, :, cols] = dot(ups[1], x, TN)
            ou[e, :, cols] = dot(ups[2], x, TN)
            od[e, :, cols] = dot(ups[0], gated, TN)
    stores = [
        pltpu.make_async_copy(src, dst, out_sem.at[n])
        for n, (src, dst) in enumerate(
            (
                (og, gg_hbm),
                (ou, gu_hbm),
                (od, gd_hbm),
                (mixed, mixed_hbm),
                (gtok, gtok_hbm),
            )
        )
    ]
    for store in stores[:3]:
        store.start()

    wait_recv(back_r.at[pl.ds(0, n_h - 1)], zb_sem)
    sums = dot(sel[...], back_r[...].reshape(total, LANES))
    at = [sums[n * toks : (n + 1) * toks] for n in range(8)]
    gtok[:, :LANES] = at[0].astype(BF)
    gtok[:, LANES:] = at[1].astype(BF)
    mixed[:, :LANES] = (at[2] + at[4] + at[6]).astype(BF)
    mixed[:, LANES:] = (at[3] + at[5] + at[7]).astype(BF)

    for store in stores[3:]:
        store.start()

    for ref, sem in sent:
        wait_send(ref, sem)
    for store in stores:
        store.wait()


def hand_over(a, b, c, d, e, ao, bo, co, do, eo, av, bv, cv, dv, ev, get_sem, put_sem):
    gets, puts = [], []
    for n, (src, held, dst) in enumerate(
        ((a, av, ao), (b, bv, bo), (c, cv, co), (d, dv, do), (e, ev, eo))
    ):
        gets.append(pltpu.make_async_copy(src, held, get_sem.at[n]))
        puts.append(pltpu.make_async_copy(held, dst, put_sem.at[n]))
    for get in gets:
        get.start()
    for get, put in zip(gets, puts, strict=True):
        get.wait()
        put.start()
    for put in puts:
        put.wait()


def layer(tokens, grad_mixed, expert_ids, gate_weight, w_gate, w_up, w_down):
    expert_ids, gate_weight = expert_ids.T, gate_weight.T
    w_gate, w_up = jnp.swapaxes(w_gate, 1, 2), jnp.swapaxes(w_up, 1, 2)
    n_g, n_j, n_h = (lax.axis_size(a) for a in ("group", "ingroup", "hid"))
    per, units, d_model = w_gate.shape
    top, toks = expert_ids.shape
    depth = min(8, n_h // 2)
    chunks = n_h // depth
    rows = depth * CAP
    width = 2 * LANES
    m = chunks * rows
    share = d_model // n_g
    hbm = pl.BlockSpec(memory_space=pl.ANY)
    block = (chunks, 2, per, rows, width)
    dma = pltpu.SemaphoreType.DMA
    outs = pl.pallas_call(
        functools.partial(kernel, (n_g, n_j, n_h, chunks, depth, per, top)),
        out_shape=(
            jax.ShapeDtypeStruct((toks, width), BF),
            jax.ShapeDtypeStruct((toks, width), BF),
            jax.ShapeDtypeStruct((per, units, share), F32),
            jax.ShapeDtypeStruct((per, units, share), F32),
            jax.ShapeDtypeStruct((per, units, share), F32),
        ),
        in_specs=[hbm] * 7,
        out_specs=(hbm,) * 5,
        scratch_shapes=[
            pltpu.VMEM((top, toks), jnp.int32),
            pltpu.VMEM((top, toks), F32),
            pltpu.VMEM((toks, width), BF),
            pltpu.VMEM((toks, width), BF),
            pltpu.VMEM(w_gate.shape, BF),
            pltpu.VMEM(w_up.shape, BF),
            pltpu.VMEM(w_down.shape, BF),
            pltpu.VMEM((8 * toks, n_h * 16), BF),
            pltpu.VMEM((depth * 16, depth * 16), BF),
            pltpu.VMEM((depth * 16, depth * 16), BF),
            pltpu.VMEM((n_h, 16, LANES), BF),
            pltpu.VMEM((n_h, 16, LANES), BF),
            pltpu.VMEM((n_h // 2, 16, LANES), BF),
            pltpu.VMEM((n_j, *block), BF),
            pltpu.VMEM((n_j, *block), BF),
            pltpu.VMEM((n_j // 2, *block), BF),
            pltpu.VMEM((n_j // 2, *block), BF),
            pltpu.VMEM((n_j // 2 - 1, *block), BF),
            pltpu.VMEM((n_h, 16, LANES), BF),
            pltpu.VMEM((n_h, 16, LANES), BF),
            pltpu.VMEM((n_g, 2, *block), BF),
            pltpu.VMEM((n_g, 3, m, per * units), BF),
            pltpu.VMEM((toks, width), BF),
            pltpu.VMEM((toks, width), BF),
            pltpu.VMEM((per, units, share), F32),
            pltpu.VMEM((per, units, share), F32),
            pltpu.VMEM((per, units, share), F32),
            dma((7,)),
            dma((5,)),
            dma((10,)),
            dma((chunks,)),
            dma((chunks,)),
            dma((chunks,)),
            dma,
            dma((chunks,)),
            dma((chunks,)),
            dma,
            dma,
            dma,
            dma,
        ],
        compiler_params=pltpu.CompilerParams(
            collective_id=0, has_side_effects=True, vmem_limit_bytes=60 * 2**20
        ),
    )(expert_ids, gate_weight, tokens, grad_mixed, w_gate, w_up, w_down)
    mixed, gtok, gg, gu, gd = pl.pallas_call(
        hand_over,
        out_shape=tuple(jax.ShapeDtypeStruct(o.shape, o.dtype) for o in outs),
        in_specs=[hbm] * 5,
        out_specs=(hbm,) * 5,
        scratch_shapes=[*(pltpu.VMEM(o.shape, o.dtype) for o in outs), dma((5,)), dma((5,))],
    )(*outs)
    return mixed, gtok, jnp.swapaxes(gg, 1, 2), jnp.swapaxes(gu, 1, 2), gd


def solution(mesh):
    both = P(("group", "hid"), None)
    return jax.shard_map(
        layer,
        mesh=mesh,
        in_specs=(
            both,
            both,
            both,
            both,
            P("hid", None, "ingroup"),
            P("hid", None, "ingroup"),
            P("hid", "ingroup", None),
        ),
        out_specs=(
            P(("group", "hid"), "ingroup"),
            P(("group", "hid"), "ingroup"),
            P("hid", "group", "ingroup"),
            P("hid", "group", "ingroup"),
            P("hid", "ingroup", "group"),
        ),
        check_vma=False,
    )
```
